128 devices in a mesh: blk: 32 (over z, x, y_hi), sub: 4 (over y_lo, core).
Axes of the slice: x: 4, y: 4 (y_hi: 2, y_lo: 2; y = y_hi * 2 + y_lo), z: 4, core: 2. Of those that a mesh axis runs over, the one named last changes fastest.
Arguments:
- features: bfloat16 [49152, 768], P(('blk', 'sub')), may hold values from -6 to 6
- scales: bfloat16 [49152], P('blk'), may hold values from 0.5 to 4
- neighbor_lists: int32 [9, 16, 49152], P(None, None, 'blk'), may hold values from 0 to 1535, as said below
- eigen_block: float32 [64, 49152], P(None, ('blk', 'sub')), may hold values from -6 to 6
Outputs:
- embedding: float32 [64, 49152], P(None, ('blk', 'sub'))
The draws below stay inside these ranges and needn't reach their ends.
Inputs may be any that keep to these rules, and one draw needn't show every extreme that they name: For each j and point p, the 16 entries neighbor_lists[j, :, p] are distinct positions within the row block that lies j - 4 blocks before p's block, counted cyclically.
All inputs are finite; a program needn't handle non-finite values.
Results may differ from the reference program's by a relative error of at most 0.0039.
Values may be sent and summed in bfloat16 or wider, within the bound.
No kernel may reach another device: no remote copies, remote signals or barrier semaphores. Data moves between devices by JAX's collectives and lax.ppermute only.
A program may use at most 128 MiB of HBM per device.

```python
import math
import jax
import jax.numpy as jnp
from jax import lax

F = 768
EIG = 64
HALF = 4
NNB = 16
SHIFTS = 9
BLOCK = 1536
NTOT = 49152
N_BLK = 32


def draw_neighbor_lists(key, part):
    key_start, key_gaps = jax.random.split(jax.random.fold_in(key, 7))
    start = jax.random.randint(key_start, (SHIFTS, 1, NTOT), 0, BLOCK)
    gaps = jax.random.randint(key_gaps, (SHIFTS, NNB, NTOT), 1, BLOCK // NNB)
    offsets = jnp.cumsum(gaps, axis=1) - gaps[:, :1, :]
    return ((start + offsets) % BLOCK).astype(jnp.int32)


def draw_features(key, part):
    key_centre, key_label, key_noise = jax.random.split(jax.random.fold_in(key, 11), 3)
    labels = jax.random.randint(key_label, (NTOT,), 0, EIG)
    centres = jax.random.normal(key_centre, (EIG, F), jnp.float32)
    noise = jax.random.normal(key_noise, (NTOT, F), jnp.float32)
    values = 0.8 * centres[labels] + 0.6 * noise
    return jnp.clip(values, -6.0, 6.0).astype(jnp.bfloat16)


def steps_of(own_key, shape, pieces, least, largest):
    loudness = 1.0
    for axis_at, blocks in pieces:
        heights = jax.random.uniform(jax.random.fold_in(jax.random.fold_in(own_key, 6), axis_at), (blocks,), jnp.float32, least / len(pieces), largest / len(pieces))
        loudness = loudness * jnp.repeat(jnp.exp(heights), shape[axis_at] // blocks).reshape((-1,) + (1,) * (len(shape) - 1 - axis_at))
    return loudness


def normal_values(key, extent, scale, limit, cuts=(), kind=jnp.bfloat16):
    factor_of = steps_of(key, extent, cuts, -0.22, 0.18) if cuts else 1.0
    drawn = jax.random.normal(key, extent, jnp.float32) * scale * factor_of
    return jnp.minimum(jnp.maximum(drawn, -limit), limit).astype(kind)


def setup_inputs(seed: int = 0) -> dict:
    arg_keys = jax.random.split(jax.random.key(seed), 5)
    features = draw_features(jax.random.fold_in(arg_keys[4], 71), 0)
    scales = jnp.clip(jnp.exp(math.log(4.0) - 2.0794415 * jax.random.uniform(arg_keys[1], (NTOT,), jnp.float32) ** steps_of(arg_keys[1], (NTOT,), ((0, 32),), -0.2, 0.2)), 0.5, 4.0).astype(jnp.bfloat16)
    neighbor_lists = draw_neighbor_lists(jax.random.fold_in(arg_keys[4], 71), 0)
    eigen_block = normal_values(arg_keys[3], (EIG, NTOT), 1.0, 6.0, ((1, 128),), jnp.float32)
    return dict(features=features, scales=scales, neighbor_lists=neighbor_lists, eigen_block=eigen_block)


def reference(features, scales, neighbor_lists, eigen_block):
    total = features.shape[0]
    feats = features.astype(jnp.float32)
    norms = lax.optimization_barrier(jnp.sum(feats * feats, axis=1))
    spread = scales.astype(jnp.float32)
    points = jnp.arange(total, dtype=jnp.int32)
    home = (points // BLOCK).astype(jnp.int32)

    def one_list(flat):
        shift_index = flat // NNB
        member = flat % NNB
        offset = shift_index - HALF
        listed = neighbor_lists[shift_index, member].astype(jnp.int32)
        partner = ((home - offset) % N_BLK * BLOCK + listed).astype(jnp.int32)
        inner = lax.optimization_barrier(jnp.sum(feats * feats[partner], axis=1))
        distance = norms + norms[partner] - 2.0 * inner
        return (jnp.exp(-distance / (F * spread * spread[partner])), partner)
    affinity, partners = lax.map(one_list, jnp.arange(SHIFTS * NNB, dtype=jnp.int32))
    row_deg = lax.optimization_barrier(jnp.sum(affinity, axis=0))
    col_deg = jax.ops.segment_sum(affinity.reshape(-1), partners.reshape(-1), num_segments=total)
    degree = 1.0 + 0.5 * (row_deg + col_deg)
    inv_root = lax.rsqrt(degree)
    scaled = eigen_block * inv_root[None, :]
    scaled_low = lax.optimization_barrier(scaled.astype(jnp.bfloat16)).astype(jnp.float32)
    weights_low = lax.optimization_barrier(affinity.astype(jnp.bfloat16)).astype(jnp.float32)

    def accumulate(carry, items):
        row_side, col_side = carry
        weight, partner_row = items
        row_side = row_side + weight[None, :] * scaled_low[:, partner_row]
        spread_terms = jax.ops.segment_sum((weight[None, :] * scaled_low).T, partner_row, num_segments=total)
        return ((row_side, col_side + spread_terms.T), None)
    zeros = jnp.zeros_like(scaled)
    sides, unused = lax.scan(accumulate, (zeros, zeros), (weights_low, partners))
    mixed = inv_root[None, :] * (scaled + 0.5 * (sides[0] + sides[1]))
    gram = jnp.dot(mixed.astype(jnp.float32), mixed.T.astype(jnp.float32), precision=lax.Precision.HIGHEST, preferred_element_type=jnp.float32)
    lower = jnp.linalg.cholesky(gram)
    return math.sqrt(total) * jax.scipy.linalg.solve_triangular(lower, mixed, lower=True)
```

```python
import functools
import math

import jax
import jax.numpy as jnp
from jax import lax
from jax.experimental import pallas as pl
from jax.experimental.pallas import tpu as pltpu
from jax.sharding import PartitionSpec as P

F = 768
ROWS = 384
SLOTS = 4
EIG = 64
NNB = 16
BAND = ((1, 2), (-2, 0), (-3, 2), (4, 0))
FOLDED = 2.0 * math.log2(math.e) / F
NT = (((1,), (1,)), ((), ()))
LIMIT = 48 * 1024 * 1024


def moved(value, blocks, flip):
    n_blk, n_sub = lax.axis_size("blk"), lax.axis_size("sub")
    pairs = [
        (b * n_sub + s, ((b + blocks) % n_blk) * n_sub + (s ^ flip))
        for b in range(n_blk)
        for s in range(n_sub)
    ]
    return lax.ppermute(value, ("blk", "sub"), pairs)


def call(body, outs, scratch=(), flops=10**9, smem=0):
    vmem = pl.BlockSpec(memory_space=pltpu.VMEM)

    def run(*args):
        specs = [pl.BlockSpec(memory_space=pltpu.SMEM)] * smem + [vmem] * (len(args) - smem)
        return pl.pallas_call(
            body,
            out_shape=outs,
            in_specs=specs,
            out_specs=jax.tree.map(lambda _: vmem, outs),
            scratch_shapes=list(scratch),
            compiler_params=pltpu.CompilerParams(vmem_limit_bytes=LIMIT),
            cost_estimate=pl.CostEstimate(flops=flops, bytes_accessed=4 * 10**6, transcendentals=0),
        )(*args)

    return run


def f32(*shape):
    return jax.ShapeDtypeStruct(shape, jnp.float32)


def bf16(*shape):
    return jax.ShapeDtypeStruct(shape, jnp.bfloat16)


def norms_kernel(f0, f1, f2, f3, out):
    ones = jnp.ones((8, F), jnp.bfloat16)
    for slot, ref in enumerate((f0, f1, f2, f3)):
        value = ref[...].astype(jnp.float32)
        square = value * value
        high = square.astype(jnp.bfloat16)
        low = (square - high.astype(jnp.float32)).astype(jnp.bfloat16)
        total = lax.dot_general(ones, high, NT, preferred_element_type=jnp.float32)
        total = total + lax.dot_general(ones, low, NT, preferred_element_type=jnp.float32)
        out[slot : slot + 1, :] = total[0:1, :]


def tile_kernel(flip, reverse, sub, f0, f1, f2, f3, moving, norms, scales, lists, aux, tile, row, col, inner, words, cols):
    me = sub[0]
    feats = moving[...].astype(jnp.float32)
    half_norm = 0.5 * jnp.sum(feats * feats, axis=1, keepdims=True)

    block_scale = aux[16:17, :]
    pieces = []
    if reverse:
        position = aux[0:16, :].astype(jnp.int32)
        group = position >> 7
        slice_at = (group * 11) >> 5
        group = (slice_at ^ me) * 3 + group - 3 * slice_at
        pieces = [(position & 127).astype(jnp.float32), jnp.left_shift(1, group).astype(jnp.float32)]
    else:
        pieces = [jnp.zeros((32, ROWS), jnp.float32)]
    stacked = jnp.concatenate(
        pieces + [FOLDED / block_scale, jnp.zeros((95, ROWS), jnp.float32)], axis=0
    )
    turned = stacked.T
    move_scale = turned[:, 32:33]
    if reverse:
        lane = lax.broadcasted_iota(jnp.int32, (64, 128), 1).astype(jnp.float32)
        for at in range(0, ROWS, 64):
            part = turned[at : at + 64]
            word = jnp.zeros((64, 128), jnp.float32)
            for m in range(NNB):
                word = word + jnp.where(part[:, m : m + 1] == lane, part[:, 16 + m : 17 + m], 0.0)
            words[at : at + 64, :] = word.astype(jnp.int32)

    row_at = lax.broadcasted_iota(jnp.int32, (8, ROWS), 0)
    for slot, ref in enumerate((f0, f1, f2, f3)):
        inner[...] = lax.dot_general(moving[...], ref[...], NT, preferred_element_type=jnp.float32)
        start = pl.multiple_of((me ^ slot) * ROWS, 128)
        listed = lists[:, pl.ds(start, ROWS)] - (me ^ flip) * ROWS
        inside = (listed >= 0) & (listed < ROWS)
        sublane = listed & 7
        bit = jnp.where(inside, listed >> 3, 0)
        first = jnp.where(inside & (bit < 24), jnp.left_shift(1, bit), 0)
        second = jnp.where(inside & (bit >= 24), jnp.left_shift(1, jnp.maximum(bit - 24, 0)), 0)
        low = jnp.zeros((8, ROWS), jnp.int32)
        high = jnp.zeros((8, ROWS), jnp.int32)
        for m in range(NNB):
            same = sublane[m : m + 1, :] == row_at
            low = low | jnp.where(same, first[m : m + 1, :], 0)
            high = high | jnp.where(same, second[m : m + 1, :], 0)
        norm = 0.5 * norms[slot : slot + 1, :]
        scale = 1.0 / scales[:, pl.ds(start, ROWS)]
        row_sum = jnp.zeros((8, ROWS), jnp.float32)
        step = 32
        for at in range(0, ROWS, step):
            source = low if at < 192 else high
            counts = [
                (source >> ((at // 8 + c) % 24)) & 1 for c in range(step // 8)
            ]
            count = jnp.concatenate(counts, axis=0)
            if reverse:
                word = words[at : at + step, :]
                count = count + jnp.concatenate(
                    [(word >> (3 * slot + g)) & 1 for g in range(3)], axis=1
                )
            power = inner[at : at + step, :] - half_norm[at : at + step] - norm
            power = power * move_scale[at : at + step] * scale
            weight = jnp.exp2(power) * count.astype(jnp.float32)
            tile[at : at + step, slot * ROWS : (slot + 1) * ROWS] = weight.astype(jnp.bfloat16)
            for c in range(step // 8):
                row_sum = row_sum + weight[8 * c : 8 * c + 8, :]
            lanes = weight[:, 0:128] + weight[:, 128:256] + weight[:, 256:384]
            if slot == 0:
                cols[at : at + step, :] = lanes
            else:
                cols[at : at + step, :] = cols[at : at + step, :] + lanes
        row[slot : slot + 1, :] = jnp.sum(row_sum, axis=0, keepdims=True)
    col[...] = jnp.sum(cols[...].T, axis=0, keepdims=True)


def col_kernel(e0, e1, e2, e3, root, t0, t1, t2, t3, t4, z0, z1, z2, z3, z4):
    block = jnp.concatenate(
        [(ref[...] * root[slot : slot + 1, :]).astype(jnp.bfloat16) for slot, ref in enumerate((e0, e1, e2, e3))],
        axis=1,
    )
    for tile, out in ((t1, z1), (t2, z2), (t3, z3), (t4, z4), (t0, z0)):
        out[...] = lax.dot_general(block, tile[...], NT, preferred_element_type=jnp.float32).astype(out.dtype)


def row_kernel(x0, x1, x2, x3, x4, t0, t1, t2, t3, t4, kept, sent):
    for half, out in ((1, sent), (0, kept)):
        at = half * 2 * ROWS
        total = jnp.zeros((EIG, 2 * ROWS), jnp.float32)
        for vectors, tile in ((x0, t0), (x1, t1), (x2, t2), (x3, t3), (x4, t4)):
            total = total + jnp.dot(
                vectors[...], tile[:, at : at + 2 * ROWS], preferred_element_type=jnp.float32
            )
        out[...] = total.astype(out.dtype)


def mix_kernel(own, root, y0, y1, y2, z0, z1, z2, z3, z4, mixed, gram):
    sides = y0[...] + y1[...].astype(jnp.float32) + y2[...] + z0[...]
    for part in (z1, z2, z3, z4):
        sides = sides + part[...].astype(jnp.float32)
    inv = root[0:1, :]
    value = inv * (own[...] * inv + 0.5 * sides)
    mixed[...] = value
    gram[...] = lax.dot_general(
        value, value, NT, precision=lax.Precision.HIGHEST, preferred_element_type=jnp.float32
    )


def solve_kernel(factor, gram, mixed, out):
    rows = lax.broadcasted_iota(jnp.int32, (EIG, 2 * EIG), 0)
    lanes = lax.broadcasted_iota(jnp.int32, (EIG, 2 * EIG), 1)
    unit = (rows + EIG == lanes).astype(jnp.float32)
    work = jnp.concatenate([gram[...], jnp.zeros((EIG, EIG), jnp.float32)], axis=1) + unit
    done = []
    for j in range(EIG):
        pivot = work[j : j + 1, :]
        root = lax.rsqrt(jnp.broadcast_to(pivot[:, j : j + 1], (1, 2 * EIG)))
        pivot = pivot * root
        done.append(pivot)
        if j + 1 < EIG:
            lower = jnp.broadcast_to(work[:, j : j + 1], (EIG, 2 * EIG)) * root
            work = work - lower * pivot
    inverse = jnp.concatenate(done, axis=0)[:, EIG:]
    out[...] = factor * jnp.dot(
        inverse, mixed[...], precision=lax.Precision.HIGHEST, preferred_element_type=jnp.float32
    )


def local(features, scales, neighbor_lists, eigen_block):
    sub = lax.axis_index("sub").astype(jnp.int32)
    half = (neighbor_lists.shape[0] - 1) // 2
    total_rows = ROWS * lax.axis_size("blk") * lax.axis_size("sub")
    sub_arg = sub.reshape(1)

    own_lists = lax.dynamic_slice_in_dim(neighbor_lists, sub * ROWS, ROWS, axis=2)
    own_scale = lax.dynamic_slice_in_dim(scales, sub * ROWS, ROWS).astype(jnp.float32)
    aux = jnp.concatenate(
        [
            own_lists.astype(jnp.float32),
            jnp.broadcast_to(own_scale[None, None, :], (2 * half + 1, 8, ROWS)),
        ],
        axis=1,
    )
    block_scales = scales.astype(jnp.float32)[None, :]

    slot2 = moved(features, 0, 2)
    slices = [moved(features, d, u) for d, u in BAND]
    side = [moved(aux[half - d], d, u) for d, u in BAND]
    slot1 = moved(features, 0, 1)
    slot3 = moved(slot2, 0, 1)
    block = (features, slot1, slot2, slot3)
    norms = call(norms_kernel, f32(SLOTS, ROWS))(*block)

    tile_outs = (bf16(ROWS, SLOTS * ROWS), f32(SLOTS, ROWS), f32(1, ROWS))
    scratch = (
        pltpu.VMEM((ROWS, ROWS), jnp.float32),
        pltpu.VMEM((ROWS, 128), jnp.int32),
        pltpu.VMEM((ROWS, 128), jnp.float32),
    )
    tiles, rows, cols = [], [], []
    work = [((0, 0), features, aux[half])] + list(zip(BAND, slices, side))
    for index, ((d, u), moving, extra) in enumerate(work):
        body = functools.partial(tile_kernel, u, index > 0)
        tile, row, col = call(body, tile_outs, scratch, 3 * 10**9, 1)(
            sub_arg, *block, moving, norms, block_scales, neighbor_lists[half + d], extra
        )
        tiles.append(tile)
        rows.append(row)
        cols.append(col if index == 0 else moved(col, -d, u))

    e1 = moved(eigen_block, 0, 1)
    e2 = moved(eigen_block, 0, 2)
    e3 = moved(e2, 0, 1)

    own_cols = functools.reduce(jnp.add, cols)
    sums = functools.reduce(jnp.add, rows)
    sums = jnp.concatenate([sums[0:1] + own_cols, sums[1:]], axis=0)
    other = moved(sums, 0, 1)
    sums = sums + jnp.concatenate([other[1:2], other[0:1], other[3:4], other[2:3]], axis=0)
    other = moved(sums, 0, 2)
    sums = sums + jnp.concatenate([other[2:4], other[0:2]], axis=0)
    root = lax.rsqrt(1.0 + 0.5 * sums)
    scaled_low = (eigen_block * root[0:1]).astype(jnp.bfloat16)
    vectors = [moved(scaled_low, d, u) for d, u in BAND]

    z_outs = (f32(EIG, ROWS),) + (bf16(EIG, ROWS),) * 4
    z = call(col_kernel, z_outs, (), 10**9)(eigen_block, e1, e2, e3, root, *tiles)
    back = [moved(part, -d, u) for (d, u), part in zip(BAND, z[1:])]
    kept, sent = call(row_kernel, (f32(EIG, 2 * ROWS), bf16(EIG, 2 * ROWS)), (), 10**9)(
        scaled_low, *vectors, *tiles
    )
    got = moved(sent, 0, 2)
    pair = moved(kept[:, ROWS:] + got[:, ROWS:].astype(jnp.float32), 0, 1)
    mixed, gram = call(mix_kernel, (f32(EIG, ROWS), f32(EIG, EIG)))(
        eigen_block, root, kept[:, :ROWS], got[:, :ROWS], pair, z[0], *back
    )
    flip = 1
    while flip < lax.axis_size("sub"):
        gram = gram + moved(gram, 0, flip)
        flip *= 2
    flip = 1
    n_blk, n_sub = lax.axis_size("blk"), lax.axis_size("sub")
    while flip < n_blk:
        gram = gram + lax.ppermute(gram, "blk", [(b, b ^ flip) for b in range(n_blk)])
        flip *= 2
    body = functools.partial(solve_kernel, math.sqrt(total_rows))
    return call(body, f32(EIG, ROWS))(gram, mixed)


def solution(mesh):
    placed = (P(("blk", "sub"), None), P("blk"), P(None, None, "blk"), P(None, ("blk", "sub")))
    return jax.shard_map(
        local, mesh=mesh, in_specs=placed, out_specs=P(None, ("blk", "sub")), check_vma=False
    )
```

```python
import functools
import math

import jax
import jax.numpy as jnp
from jax import lax
from jax.experimental import pallas as pl
from jax.experimental.pallas import tpu as pltpu
from jax.sharding import PartitionSpec as P

F = 768
ROWS = 384
SLOTS = 4
EIG = 64
NNB = 16
BAND = ((1, 2), (-2, 0), (3, 2), (-4, 0))
ONWARD = ((2, 0), (-2, 0))
EXTRA = 3 * NNB
FOLDED = 2.0 * math.log2(math.e) / F
NT = (((1,), (1,)), ((), ()))
LIMIT = 48 * 1024 * 1024


def moved(value, blocks, flip):
    n_blk, n_sub = lax.axis_size("blk"), lax.axis_size("sub")
    pairs = [
        (b * n_sub + s, ((b + blocks) % n_blk) * n_sub + (s ^ flip))
        for b in range(n_blk)
        for s in range(n_sub)
    ]
    return lax.ppermute(value, ("blk", "sub"), pairs)


VMEM = pl.BlockSpec(memory_space=pltpu.VMEM)
SMEM = pl.BlockSpec(memory_space=pltpu.SMEM)
HBM = pl.BlockSpec(memory_space=pltpu.HBM)


def call(body, outs, scratch=(), flops=10**9, specs=None):
    def run(*args):
        return pl.pallas_call(
            body,
            grid=(1,),
            out_shape=outs,
            in_specs=list(specs) if specs else [VMEM] * len(args),
            out_specs=jax.tree.map(lambda _: VMEM, outs),
            scratch_shapes=list(scratch),
            compiler_params=pltpu.CompilerParams(vmem_limit_bytes=LIMIT),
            cost_estimate=pl.CostEstimate(flops=flops, bytes_accessed=4 * 10**6, transcendentals=0),
        )(*args)

    return run


def f32(*shape):
    return jax.ShapeDtypeStruct(shape, jnp.float32)


def bf16(*shape):
    return jax.ShapeDtypeStruct(shape, jnp.bfloat16)


def norms_kernel(f0, f1, f2, f3, out):
    ones = jnp.ones((8, F), jnp.bfloat16)
    for slot, ref in enumerate((f0, f1, f2, f3)):
        value = ref[...].astype(jnp.float32)
        square = value * value
        high = square.astype(jnp.bfloat16)
        low = (square - high.astype(jnp.float32)).astype(jnp.bfloat16)
        total = lax.dot_general(ones, high, NT, preferred_element_type=jnp.float32)
        total = total + lax.dot_general(ones, low, NT, preferred_element_type=jnp.float32)
        out[slot : slot + 1, :] = total[0:1, :]


def pack_kernel(half, sub, features, scales, lists, first, second, held, sems, wide):
    at = pl.multiple_of(sub[0] * ROWS, 128)
    copies = [
        pltpu.make_async_copy(lists.at[half - d, :, pl.ds(at, ROWS)], held.at[index], sems.at[index])
        for index, (d, _) in enumerate(BAND)
    ]
    bulk = [
        pltpu.make_async_copy(features, out.at[:ROWS, :], wide.at[index])
        for index, out in enumerate((first, second))
    ]
    for copy in bulk + copies:
        copy.start()
    scale = jnp.concatenate([scales[:, pl.ds(at, ROWS)], jnp.ones((1, ROWS), jnp.float32)], axis=1)
    scale = jnp.broadcast_to(scale, (NNB, 2 * ROWS)).astype(jnp.bfloat16)
    for out in (first, second):
        out[ROWS + 2 * NNB :, :] = scale
    for index in range(len(BAND)):
        copies[index].wait()
        position = held[index]
        digits = jnp.concatenate([position >> 6, position & 63], axis=1)
        out = (first, second)[index % 2]
        start = ROWS + NNB * (index // 2)
        out[start : start + NNB, :] = digits.astype(jnp.float32).astype(jnp.bfloat16)
    for copy in bulk:
        copy.wait()


def tile_kernel(flip, reverse, sub, f0, f1, f2, f3, moving, norms, scales, before, lists, tile, row, col, inner, words, cols):
    me = sub[0]
    feats = moving[:ROWS, :].astype(jnp.float32)
    half_norm = 0.5 * jnp.sum(feats * feats, axis=1, keepdims=True)

    if reverse:
        digits = moving[ROWS + reverse - NNB : ROWS + reverse, :].astype(jnp.float32).astype(jnp.int32)
        position = digits[:, :ROWS] * 64 + digits[:, ROWS:]
        group = position >> 7
        slice_at = (group * 11) >> 5
        group = (slice_at ^ me) * 3 + group - 3 * slice_at
        pieces = [(position & 127).astype(jnp.float32), jnp.left_shift(1, group).astype(jnp.float32)]
        own_scale = moving[ROWS + 2 * NNB :, :ROWS].astype(jnp.float32)[0:1]
    else:
        pieces = [jnp.zeros((32, ROWS), jnp.float32)]
        own_scale = scales[:, pl.ds(pl.multiple_of(me * ROWS, 128), ROWS)]
    stacked = jnp.concatenate(
        pieces + [FOLDED / own_scale, jnp.zeros((95, ROWS), jnp.float32)], axis=0
    )
    turned = stacked.T
    move_scale = turned[:, 32:33]
    if reverse:
        lane = lax.broadcasted_iota(jnp.int32, (64, 128), 1).astype(jnp.float32)
        for at in range(0, ROWS, 64):
            part = turned[at : at + 64]
            word = jnp.zeros((64, 128), jnp.float32)
            for m in range(NNB):
                word = word + jnp.where(part[:, m : m + 1] == lane, part[:, 16 + m : 17 + m], 0.0)
            words[at : at + 64, :] = word.astype(jnp.int32)

    row_at = lax.broadcasted_iota(jnp.int32, (8, ROWS), 0)
    for slot, ref in enumerate((f0, f1, f2, f3)):
        inner[...] = lax.dot_general(moving[:ROWS, :], ref[...], NT, preferred_element_type=jnp.float32)
        start = pl.multiple_of((me ^ slot) * ROWS, 128)
        listed = lists[0, :, pl.ds(start, ROWS)] - (me ^ flip) * ROWS
        inside = (listed >= 0) & (listed < ROWS)
        sublane = listed & 7
        bit = jnp.where(inside, listed >> 3, 0)
        first = jnp.where(inside & (bit < 24), jnp.left_shift(1, bit), 0)
        second = jnp.where(inside & (bit >= 24), jnp.left_shift(1, jnp.maximum(bit - 24, 0)), 0)
        low = jnp.zeros((8, ROWS), jnp.int32)
        high = jnp.zeros((8, ROWS), jnp.int32)
        for m in range(NNB):
            same = sublane[m : m + 1, :] == row_at
            low = low | jnp.where(same, first[m : m + 1, :], 0)
            high = high | jnp.where(same, second[m : m + 1, :], 0)
        norm = 0.5 * norms[slot : slot + 1, :]
        scale = 1.0 / scales[:, pl.ds(start, ROWS)]
        row_sum = jnp.zeros((8, ROWS), jnp.float32)
        step = 32
        for at in range(0, ROWS, step):
            source = low if at < 192 else high
            counts = [
                (source >> ((at // 8 + c) % 24)) & 1 for c in range(step // 8)
            ]
            count = jnp.concatenate(counts, axis=0)
            if reverse:
                word = words[at : at + step, :]
                count = count + jnp.concatenate(
                    [(word >> (3 * slot + g)) & 1 for g in range(3)], axis=1
                )
            power = inner[at : at + step, :] - half_norm[at : at + step] - norm
            power = power * move_scale[at : at + step] * scale
            weight = jnp.exp2(power) * count.astype(jnp.float32)
            tile[at : at + step, slot * ROWS : (slot + 1) * ROWS] = weight.astype(jnp.bfloat16)
            for c in range(step // 8):
                row_sum = row_sum + weight[8 * c : 8 * c + 8, :]
            lanes = weight[:, 0:128] + weight[:, 128:256] + weight[:, 256:384]
            if slot == 0:
                cols[at : at + step, :] = lanes
            else:
                cols[at : at + step, :] = cols[at : at + step, :] + lanes
        row[slot : slot + 1, :] = before[slot : slot + 1, :] + jnp.sum(row_sum, axis=0, keepdims=True)
    col[...] = jnp.sum(cols[...].T, axis=0, keepdims=True)


def col_kernel(e0, e1, e2, e3, root, t0, t1, t2, t3, t4, z0, z1, z2, z3, z4):
    block = jnp.concatenate(
        [(ref[...] * root[slot : slot + 1, :]).astype(jnp.bfloat16) for slot, ref in enumerate((e0, e1, e2, e3))],
        axis=1,
    )
    for tile, out in ((t1, z1), (t2, z2), (t3, z3), (t4, z4), (t0, z0)):
        out[...] = lax.dot_general(block, tile[...], NT, preferred_element_type=jnp.float32).astype(out.dtype)


def row_kernel(x0, x1, x2, x3, x4, t0, t1, t2, t3, t4, kept, sent):
    for half, out in ((1, sent), (0, kept)):
        at = half * 2 * ROWS
        total = jnp.zeros((EIG, 2 * ROWS), jnp.float32)
        for vectors, tile in ((x0, t0), (x1, t1), (x2, t2), (x3, t3), (x4, t4)):
            total = total + jnp.dot(
                vectors[...], tile[:, at : at + 2 * ROWS], preferred_element_type=jnp.float32
            )
        out[...] = total.astype(out.dtype)


def mix_kernel(own, root, y0, y1, y2, z0, z1, z2, z3, z4, mixed, gram):
    sides = y0[...] + y1[...].astype(jnp.float32) + y2[...] + z0[...]
    for part in (z1, z2, z3, z4):
        sides = sides + part[...].astype(jnp.float32)
    inv = root[0:1, :]
    value = inv * (own[...] * inv + 0.5 * sides)
    mixed[...] = value
    total = lax.dot_general(
        value, value, NT, precision=lax.Precision.HIGHEST, preferred_element_type=jnp.float32
    )
    gram[...] = jnp.concatenate([total[: EIG // 2], total[EIG // 2 :]], axis=1)


def solve_kernel(factor, gram, mixed, out):
    rows = lax.broadcasted_iota(jnp.int32, (EIG, 2 * EIG), 0)
    lanes = lax.broadcasted_iota(jnp.int32, (EIG, 2 * EIG), 1)
    unit = (rows + EIG == lanes).astype(jnp.float32)
    square = jnp.concatenate([gram[:, :EIG], gram[:, EIG:]], axis=0)
    work = jnp.concatenate([square, jnp.zeros((EIG, EIG), jnp.float32)], axis=1) + unit
    done = []
    for j in range(EIG):
        pivot = work[j : j + 1, :]
        root = lax.rsqrt(jnp.broadcast_to(pivot[:, j : j + 1], (1, 2 * EIG)))
        pivot = pivot * root
        done.append(pivot)
        if j + 1 < EIG:
            lower = jnp.broadcast_to(work[:, j : j + 1], (EIG, 2 * EIG)) * root
            work = work - lower * pivot
    inverse = jnp.concatenate(done, axis=0)[:, EIG:]
    out[...] = factor * jnp.dot(
        inverse, mixed[...], precision=lax.Precision.HIGHEST, preferred_element_type=jnp.float32
    )


def local(features, scales, neighbor_lists, eigen_block):
    sub = lax.axis_index("sub").astype(jnp.int32)
    half = (neighbor_lists.shape[0] - 1) // 2
    total_rows = ROWS * lax.axis_size("blk") * lax.axis_size("sub")
    sub_arg = sub.reshape(1)

    block_scales = scales.astype(jnp.float32)[None, :]
    first, second = call(
        functools.partial(pack_kernel, half),
        (bf16(ROWS + EXTRA, F),) * 2,
        (
            pltpu.VMEM((len(BAND), NNB, ROWS), jnp.int32),
            pltpu.SemaphoreType.DMA((len(BAND),)),
            pltpu.SemaphoreType.DMA((2,)),
        ),
        10**7,
        (SMEM, HBM, VMEM, HBM),
    )(sub_arg, features, block_scales, neighbor_lists)

    first, second, ready = lax.optimization_barrier((first, second, features))
    first = moved(first, *BAND[0])
    second = moved(second, *BAND[1])
    slot2 = moved(ready, 0, 2)
    slot1 = moved(ready, 0, 1)
    third = moved(first, *ONWARD[0])
    fourth = moved(second, *ONWARD[1])
    slot3 = moved(slot2, 0, 1)
    block = (features, slot1, slot2, slot3)
    norms = call(norms_kernel, f32(SLOTS, ROWS))(*block)

    tile_outs = (bf16(ROWS, SLOTS * ROWS), f32(SLOTS, ROWS), f32(1, ROWS))
    scratch = (
        pltpu.VMEM((ROWS, ROWS), jnp.float32),
        pltpu.VMEM((ROWS, 128), jnp.int32),
        pltpu.VMEM((ROWS, 128), jnp.float32),
    )
    row = jnp.zeros((SLOTS, ROWS), jnp.float32)
    tiles, cols = [], []
    work = [((0, 0), features)] + list(zip(BAND, (first, second, third, fourth)))
    for index, ((d, u), moving) in enumerate(work):
        body = functools.partial(tile_kernel, u, NNB * ((index + 1) // 2))
        listed = pl.BlockSpec((1, NNB, SLOTS * ROWS), lambda i, at=half + d: (at, 0, 0))
        tile, row, col = call(
            body, tile_outs, scratch, 3 * 10**9, (SMEM,) + (VMEM,) * 8 + (listed,)
        )(sub_arg, *block, moving, norms, block_scales, row, neighbor_lists)
        tiles.append(tile)
        cols.append(col if index == 0 else moved(col, -d, u))

    e1 = moved(eigen_block, 0, 1)
    e2 = moved(eigen_block, 0, 2)
    e3 = moved(e2, 0, 1)

    pair = row[0:2] + moved(row[2:4], 0, 2)
    own = pair[0:1] + moved(pair[1:2], 0, 1)
    root = lax.rsqrt(1.0 + 0.5 * (own + functools.reduce(jnp.add, cols)))
    scaled_low = (eigen_block * root).astype(jnp.bfloat16)
    vectors = [moved(scaled_low, d, u) for d, u in BAND]
    root = jnp.concatenate([root, moved(root, 0, 1)], axis=0)
    root = jnp.concatenate([root, moved(root, 0, 2)], axis=0)

    z_outs = (f32(EIG, ROWS),) + (bf16(EIG, ROWS),) * 4
    z = call(col_kernel, z_outs, (), 10**8)(eigen_block, e1, e2, e3, root, *tiles)
    back = [moved(part, -d, u) for (d, u), part in zip(BAND, z[1:])]
    vectors, _ = lax.optimization_barrier((vectors, z[0]))
    kept, sent = call(row_kernel, (f32(EIG, 2 * ROWS), bf16(EIG, 2 * ROWS)), (), 10**9)(
        scaled_low, *vectors, *tiles
    )
    got = moved(sent, 0, 2)
    pair = moved(kept[:, ROWS:] + got[:, ROWS:].astype(jnp.float32), 0, 1)
    mixed, gram = call(mix_kernel, (f32(EIG, ROWS), f32(EIG // 2, 2 * EIG)))(
        eigen_block, root, kept[:, :ROWS], got[:, :ROWS], pair, z[0], *back
    )
    flip = 1
    while flip < lax.axis_size("sub"):
        gram = gram + moved(gram, 0, flip)
        flip *= 2
    flip = 1
    n_blk, n_sub = lax.axis_size("blk"), lax.axis_size("sub")
    while flip < n_blk:
        gram = gram + lax.ppermute(gram, "blk", [(b, b ^ flip) for b in range(n_blk)])
        flip *= 2
    body = functools.partial(solve_kernel, math.sqrt(total_rows))
    return call(body, f32(EIG, ROWS))(gram, mixed)


def solution(mesh):
    placed = (P(("blk", "sub"), None), P("blk"), P(None, None, "blk"), P(None, ("blk", "sub")))
    return jax.shard_map(
        local, mesh=mesh, in_specs=placed, out_specs=P(None, ("blk", "sub")), check_vma=False
    )
```

```python
import functools
import math

import jax
import jax.numpy as jnp
from jax import lax
from jax.experimental import pallas as pl
from jax.experimental.pallas import tpu as pltpu
from jax.sharding import PartitionSpec as P

F = 768
ROWS = 384
SLOTS = 4
EIG = 64
NNB = 16
BAND = ((1, 2), (-2, 0), (3, 2), (-4, 0))
ONWARD = ((2, 0), (-2, 0))
EXTRA = 3 * NNB
ROUNDS = ((0, 1), (0, 2), (1, 2), (2, 0), (6, 0), (8, 0), (24, 0))
FOLDED = 2.0 * math.log2(math.e) / F
NT = (((1,), (1,)), ((), ()))
LIMIT = 24 * 1024 * 1024


def moved(value, blocks, flip):
    n_blk, n_sub = lax.axis_size("blk"), lax.axis_size("sub")
    pairs = [
        (b * n_sub + s, ((b + blocks) % n_blk) * n_sub + (s ^ flip))
        for b in range(n_blk)
        for s in range(n_sub)
    ]
    return lax.ppermute(value, ("blk", "sub"), pairs)


VMEM = pl.BlockSpec(memory_space=pltpu.VMEM)
SMEM = pl.BlockSpec(memory_space=pltpu.SMEM)
HBM = pl.BlockSpec(memory_space=pltpu.HBM)


def call(body, outs, scratch=(), specs=None, flops=1000):
    def run(*args):
        return pl.pallas_call(
            body,
            grid=(1,),
            out_shape=outs,
            in_specs=list(specs) if specs else [VMEM] * len(args),
            out_specs=jax.tree.map(lambda _: VMEM, outs),
            scratch_shapes=list(scratch),
            compiler_params=pltpu.CompilerParams(vmem_limit_bytes=LIMIT),
            cost_estimate=pl.CostEstimate(flops=flops, bytes_accessed=1000, transcendentals=0),
        )(*args)

    return run


def f32(*shape):
    return jax.ShapeDtypeStruct(shape, jnp.float32)


def bf16(*shape):
    return jax.ShapeDtypeStruct(shape, jnp.bfloat16)


def own_tile_kernel(sub, f0, f1, f2, f3, scales, lists, tile, row, col, norms, inner, words, cols):
    ones = jnp.ones((8, F), jnp.bfloat16)
    for slot, ref in enumerate((f0, f1, f2, f3)):
        value = ref[...].astype(jnp.float32)
        square = value * value
        high = square.astype(jnp.bfloat16)
        low = (square - high.astype(jnp.float32)).astype(jnp.bfloat16)
        total = lax.dot_general(ones, high, NT, preferred_element_type=jnp.float32)
        total = total + lax.dot_general(ones, low, NT, preferred_element_type=jnp.float32)
        norms[slot : slot + 1, :] = total[0:1, :]
    tile_kernel(0, 0, sub, f0, f1, f2, f3, f0, norms, scales, None, lists, tile, row, col, inner, words, cols)


def band_tile_kernel(flip, reverse, sub, *refs):
    tile_kernel(flip, reverse, sub, *refs[:8], *refs[-7:])


def pack_kernel(half, sub, features, scales, lists, first, second):
    at = pl.multiple_of(sub[0] * ROWS, 128)
    scale = jnp.concatenate([scales[:, pl.ds(at, ROWS)], jnp.ones((1, ROWS), jnp.float32)], axis=1)
    scale = jnp.broadcast_to(scale, (NNB, 2 * ROWS)).astype(jnp.bfloat16)
    for out, chosen in ((first, BAND[0::2]), (second, BAND[1::2])):
        out[:ROWS, :] = features[...]
        for index, (d, _) in enumerate(chosen):
            position = lists[half - d]
            digits = jnp.concatenate([position >> 6, position & 63], axis=1)
            start = ROWS + NNB * index
            out[start : start + NNB, :] = digits.astype(jnp.float32).astype(jnp.bfloat16)
        out[ROWS + 2 * NNB :, :] = scale


def tile_kernel(flip, reverse, sub, f0, f1, f2, f3, moving, norms, scales, before, lists, tile, row, col, inner, words, cols):
    me = sub[0]
    feats = moving[:ROWS, :].astype(jnp.float32)
    half_norm = 0.5 * jnp.sum(feats * feats, axis=1, keepdims=True)

    if reverse:
        digits = moving[ROWS + reverse - NNB : ROWS + reverse, :].astype(jnp.float32).astype(jnp.int32)
        position = digits[:, :ROWS] * 64 + digits[:, ROWS:]
        group = position >> 7
        slice_at = (group * 11) >> 5
        group = (slice_at ^ me) * 3 + group - 3 * slice_at
        pieces = [(position & 127).astype(jnp.float32), jnp.left_shift(1, group).astype(jnp.float32)]
        own_scale = moving[ROWS + 2 * NNB :, :ROWS].astype(jnp.float32)[0:1]
    else:
        pieces = [jnp.zeros((32, ROWS), jnp.float32)]
        own_scale = scales[:, pl.ds(pl.multiple_of(me * ROWS, 128), ROWS)]
    stacked = jnp.concatenate(
        pieces + [FOLDED / own_scale, jnp.zeros((95, ROWS), jnp.float32)], axis=0
    )
    turned = stacked.T
    move_scale = turned[:, 32:33]
    if reverse:
        lane = lax.broadcasted_iota(jnp.int32, (64, 128), 1).astype(jnp.float32)
        for at in range(0, ROWS, 64):
            part = turned[at : at + 64]
            word = jnp.zeros((64, 128), jnp.float32)
            for m in range(NNB):
                word = word + jnp.where(part[:, m : m + 1] == lane, part[:, 16 + m : 17 + m], 0.0)
            words[at : at + 64, :] = word.astype(jnp.int32)

    row_at = lax.broadcasted_iota(jnp.int32, (8, ROWS), 0)
    for slot, ref in enumerate((f0, f1, f2, f3)):
        inner[slot] = lax.dot_general(moving[:ROWS, :], ref[...], NT, preferred_element_type=jnp.float32)
        start = pl.multiple_of((me ^ slot) * ROWS, 128)
        listed = lists[0, :, pl.ds(start, ROWS)] - (me ^ flip) * ROWS
        inside = (listed >= 0) & (listed < ROWS)
        sublane = listed & 7
        bit = jnp.where(inside, listed >> 3, 0)
        first = jnp.where(inside & (bit < 24), jnp.left_shift(1, bit), 0)
        second = jnp.where(inside & (bit >= 24), jnp.left_shift(1, jnp.maximum(bit - 24, 0)), 0)
        low = jnp.zeros((8, ROWS), jnp.int32)
        high = jnp.zeros((8, ROWS), jnp.int32)
        for m in range(NNB):
            same = sublane[m : m + 1, :] == row_at
            low = low | jnp.where(same, first[m : m + 1, :], 0)
            high = high | jnp.where(same, second[m : m + 1, :], 0)
        norm = 0.5 * norms[slot : slot + 1, :]
        scale = 1.0 / scales[:, pl.ds(start, ROWS)]
        row_sum = jnp.zeros((8, ROWS), jnp.float32)
        step = 32
        for at in range(0, ROWS, step):
            source = low if at < 192 else high
            counts = [
                (source >> ((at // 8 + c) % 24)) & 1 for c in range(step // 8)
            ]
            count = jnp.concatenate(counts, axis=0)
            if reverse:
                word = words[at : at + step, :]
                count = count + jnp.concatenate(
                    [(word >> (3 * slot + g)) & 1 for g in range(3)], axis=1
                )
            power = inner[slot, at : at + step, :] - half_norm[at : at + step] - norm
            power = power * move_scale[at : at + step] * scale
            weight = jnp.exp2(power) * count.astype(jnp.float32)
            tile[at : at + step, slot * ROWS : (slot + 1) * ROWS] = weight.astype(jnp.bfloat16)
            for c in range(step // 8):
                row_sum = row_sum + weight[8 * c : 8 * c + 8, :]
            lanes = weight[:, 0:128] + weight[:, 128:256] + weight[:, 256:384]
            if slot == 0:
                cols[at : at + step, :] = lanes
            else:
                cols[at : at + step, :] = cols[at : at + step, :] + lanes
        total = jnp.sum(row_sum, axis=0, keepdims=True)
        row[slot : slot + 1, :] = before[slot : slot + 1, :] + total if reverse else total
    col[...] = jnp.sum(cols[...].T, axis=0, keepdims=True)


def col_kernel(x0, x1, far, t0, t1, t2, t3, t4, z0, z1, z2, z3, z4):
    block = jnp.concatenate([x0[...], x1[...], far[:EIG, :], far[EIG:, :]], axis=1)
    for tile, out in ((t1, z1), (t2, z2), (t3, z3), (t4, z4), (t0, z0)):
        out[...] = lax.dot_general(block, tile[...], NT, preferred_element_type=jnp.float32).astype(out.dtype)


def row_kernel(x0, x1, x2, x3, x4, t0, t1, t2, t3, t4, y0, y2, sent):
    for slot, out, at_out in ((1, sent, 0), (3, sent, EIG), (0, y0, 0), (2, y2, 0)):
        at = slot * ROWS
        total = jnp.zeros((EIG, ROWS), jnp.float32)
        for vectors, tile in ((x0, t0), (x1, t1), (x2, t2), (x3, t3), (x4, t4)):
            total = total + jnp.dot(
                vectors[...], tile[:, at : at + ROWS], preferred_element_type=jnp.float32
            )
        out[at_out : at_out + EIG, :] = total


def mix_kernel(own, root, y0, y1, y2, z0, z1, z2, z3, z4, mixed, gram):
    sides = y0[...] + y1[:EIG, :] + y2[...].astype(jnp.float32) + z0[...]
    for part in (z1, z2, z3, z4):
        sides = sides + part[...].astype(jnp.float32)
    inv = root[0:1, :]
    value = inv * (own[...] * inv + 0.5 * sides)
    mixed[...] = value
    total = lax.dot_general(
        value, value, NT, precision=lax.Precision.HIGHEST, preferred_element_type=jnp.float32
    )
    gram[...] = jnp.concatenate([total[: EIG // 2], total[EIG // 2 :]], axis=1)


def solve_kernel(factor, gram, mixed, out):
    rows = lax.broadcasted_iota(jnp.int32, (EIG, 2 * EIG), 0)
    lanes = lax.broadcasted_iota(jnp.int32, (EIG, 2 * EIG), 1)
    unit = (rows + EIG == lanes).astype(jnp.float32)
    square = jnp.concatenate([gram[:, :EIG], gram[:, EIG:]], axis=0)
    work = jnp.concatenate([square, jnp.zeros((EIG, EIG), jnp.float32)], axis=1) + unit
    done = []
    for at in range(0, EIG, 8):
        wide = [jnp.broadcast_to(work[:, at + j : at + j + 1], (EIG - at, 2 * EIG)) for j in range(8)]
        for j in range(8):
            root = lax.rsqrt(wide[j][j : j + 1, :])
            pivot = work[j : j + 1, :] * root
            done.append(pivot)
            lower = wide[j] * root
            work = work - lower * pivot
            for other in range(j + 1, 8):
                wide[other] = wide[other] - lower * (wide[other][j : j + 1, :] * root)
        work = work[8:]
    inverse = jnp.concatenate(done, axis=0)[:, EIG:]
    out[...] = factor * jnp.dot(
        inverse, mixed[...], precision=lax.Precision.HIGHEST, preferred_element_type=jnp.float32
    )


def local(features, scales, neighbor_lists, eigen_block):
    sub = lax.axis_index("sub").astype(jnp.int32)
    half = (neighbor_lists.shape[0] - 1) // 2
    total_rows = ROWS * lax.axis_size("blk") * lax.axis_size("sub")
    sub_arg = sub.reshape(1)

    block_scales = scales.astype(jnp.float32)[None, :]
    own_lists = lax.dynamic_slice_in_dim(neighbor_lists, sub * ROWS, ROWS, axis=2)
    first, second = call(
        functools.partial(pack_kernel, half),
        (bf16(ROWS + EXTRA, F),) * 2,
        specs=(SMEM, VMEM, VMEM, VMEM),
    )(sub_arg, features, block_scales, own_lists)

    first, second, ready = lax.optimization_barrier((first, second, features))
    first = moved(first, *BAND[0])
    second = moved(second, *BAND[1])
    slot2 = moved(ready, 0, 2)
    slot1 = moved(ready, 0, 1)
    slot3 = moved(slot2, 0, 1)
    block = (features, slot1, slot2, slot3)

    tile_outs = (bf16(ROWS, SLOTS * ROWS), f32(SLOTS, ROWS), f32(1, ROWS))
    scratch = (
        pltpu.VMEM((SLOTS, ROWS, ROWS), jnp.float32),
        pltpu.VMEM((ROWS, 128), jnp.int32),
        pltpu.VMEM((ROWS, 128), jnp.float32),
    )

    def listed(d):
        return pl.BlockSpec((1, NNB, SLOTS * ROWS), lambda i: (half + d, 0, 0))

    def band_tile(index, moving, row, tokens=(), flops=1000):
        d, u = BAND[index]
        body = functools.partial(band_tile_kernel, u, NNB * (1 + index // 2))
        specs = (SMEM,) + (VMEM,) * 8 + (HBM,) * len(tokens) + (listed(d),)
        args = (sub_arg, *block, moving, norms, block_scales, row, *tokens, neighbor_lists)
        tile, row, col = call(body, tile_outs, scratch, specs, flops)(*args)
        return tile, row, moved(col, -d, u)

    tile0, row, col0, norms = call(
        own_tile_kernel,
        tile_outs + (f32(SLOTS, ROWS),),
        scratch,
        (SMEM,) + (VMEM,) * 5 + (listed(0),),
    )(sub_arg, *block, block_scales, neighbor_lists)
    first, second, row = lax.optimization_barrier((first, second, row))
    third = moved(first, *ONWARD[0])
    fourth = moved(second, *ONWARD[1])
    tile1, row, col1 = band_tile(0, first, row)
    tile2, row, col2 = band_tile(1, second, row)
    tile3, row, col3 = band_tile(2, third, row, (col1,))
    tile4, row, col4 = band_tile(3, fourth, row, (col2,), 4 * 10**9)
    tiles = (tile0, tile1, tile2, tile3, tile4)

    pair = row[0:2] + moved(row[2:4], 0, 2)
    own = pair[0:1] + moved(pair[1:2], 0, 1)
    root = lax.rsqrt(1.0 + 0.5 * (own + col0 + col1 + col2 + col3 + col4))
    scaled_low = (eigen_block * root).astype(jnp.bfloat16)
    vectors = [moved(scaled_low, d, u) for d, u in BAND]
    x1 = moved(scaled_low, 0, 1)
    far = moved(jnp.concatenate([scaled_low, x1], axis=0), 0, 2)

    z_outs = (f32(EIG, ROWS),) + (bf16(EIG, ROWS),) * 4
    z0, z1, z2, z3, z4 = call(col_kernel, z_outs)(scaled_low, x1, far, *tiles)
    back = [moved(part, -d, u) for (d, u), part in zip(BAND, (z1, z2, z3, z4))]
    vectors, _ = lax.optimization_barrier((vectors, z0))
    y_outs = (f32(EIG, ROWS), f32(EIG, ROWS), f32(2 * EIG, ROWS))
    y0, y2, sent = call(row_kernel, y_outs)(scaled_low, *vectors, *tiles)
    other = moved(sent, 0, 1)
    across = moved((y2 + other[EIG:]).astype(jnp.bfloat16), 0, 2)
    mixed, gram = call(mix_kernel, (f32(EIG, ROWS), f32(EIG // 2, 2 * EIG)))(
        eigen_block, root, y0, other, across, z0, *back
    )
    n_blk, n_sub = lax.axis_size("blk"), lax.axis_size("sub")
    for flip_blk, flip_sub in ROUNDS:
        pairs = [
            (b * n_sub + s, (b ^ flip_blk) * n_sub + (s ^ flip_sub))
            for b in range(n_blk)
            for s in range(n_sub)
        ]
        gram = gram + lax.ppermute(gram, ("blk", "sub"), pairs)
    body = functools.partial(solve_kernel, math.sqrt(total_rows))
    return call(body, f32(EIG, ROWS))(gram, mixed)


def solution(mesh):
    placed = (P(("blk", "sub"), None), P("blk"), P(None, None, "blk"), P(None, ("blk", "sub")))
    return jax.shard_map(
        local, mesh=mesh, in_specs=placed, out_specs=P(None, ("blk", "sub")), check_vma=False
    )
```

```python
import functools
import math

import jax
import jax.numpy as jnp
from jax import lax
from jax.experimental import pallas as pl
from jax.experimental.pallas import tpu as pltpu
from jax.sharding import PartitionSpec as P

F = 768
ROWS = 384
SLOTS = 4
EIG = 64
NNB = 16
BAND = ((1, 2), (-2, 0), (3, 2), (-4, 0))
ONWARD = ((2, 0), (-2, 0))
EXTRA = 3 * NNB
ROUNDS = (((0, 1),), ((0, 2), (1, 0), (1, 2)), ((2, 0), (4, 0), (6, 0)), ((8, 0), (16, 0), (24, 0)))
FOLDED = 2.0 * math.log2(math.e) / F
NT = (((1,), (1,)), ((), ()))
LIMIT = 24 * 1024 * 1024


def moved(value, blocks, flip):
    n_blk, n_sub = lax.axis_size("blk"), lax.axis_size("sub")
    pairs = [
        (b * n_sub + s, ((b + blocks) % n_blk) * n_sub + (s ^ flip))
        for b in range(n_blk)
        for s in range(n_sub)
    ]
    return lax.ppermute(value, ("blk", "sub"), pairs)


VMEM = pl.BlockSpec(memory_space=pltpu.VMEM)
SMEM = pl.BlockSpec(memory_space=pltpu.SMEM)
HBM = pl.BlockSpec(memory_space=pltpu.HBM)


def call(body, outs, scratch=(), specs=None, flops=1000):
    def run(*args):
        return pl.pallas_call(
            body,
            grid=(1,),
            out_shape=outs,
            in_specs=list(specs) if specs else [VMEM] * len(args),
            out_specs=jax.tree.map(lambda _: VMEM, outs),
            scratch_shapes=list(scratch),
            compiler_params=pltpu.CompilerParams(vmem_limit_bytes=LIMIT),
            cost_estimate=pl.CostEstimate(flops=flops, bytes_accessed=1000, transcendentals=0),
        )(*args)

    return run


def f32(*shape):
    return jax.ShapeDtypeStruct(shape, jnp.float32)


def bf16(*shape):
    return jax.ShapeDtypeStruct(shape, jnp.bfloat16)


def own_tile_kernel(sub, f0, f1, f2, f3, scales, lists, tile, row, col, norms, inner, words, cols):
    ones = jnp.ones((8, F), jnp.bfloat16)
    for slot, ref in enumerate((f0, f1, f2, f3)):
        value = ref[...].astype(jnp.float32)
        square = value * value
        high = square.astype(jnp.bfloat16)
        low = (square - high.astype(jnp.float32)).astype(jnp.bfloat16)
        total = lax.dot_general(ones, high, NT, preferred_element_type=jnp.float32)
        total = total + lax.dot_general(ones, low, NT, preferred_element_type=jnp.float32)
        norms[slot : slot + 1, :] = total[0:1, :]
    tile_kernel(0, 0, sub, f0, f1, f2, f3, f0, norms, scales, None, lists, tile, row, col, inner, words, cols)


def band_tile_kernel(flip, reverse, sub, *refs):
    tile_kernel(flip, reverse, sub, *refs[:8], *refs[-7:])


def pack_kernel(half, sub, features, scales, lists, first, second):
    at = pl.multiple_of(sub[0] * ROWS, 128)
    scale = jnp.concatenate([scales[:, pl.ds(at, ROWS)], jnp.ones((1, ROWS), jnp.float32)], axis=1)
    scale = jnp.broadcast_to(scale, (NNB, 2 * ROWS)).astype(jnp.bfloat16)
    for out, chosen in ((first, BAND[0::2]), (second, BAND[1::2])):
        out[:ROWS, :] = features[...]
        for index, (d, _) in enumerate(chosen):
            position = lists[half - d]
            digits = jnp.concatenate([position >> 6, position & 63], axis=1)
            start = ROWS + NNB * index
            out[start : start + NNB, :] = digits.astype(jnp.float32).astype(jnp.bfloat16)
        out[ROWS + 2 * NNB :, :] = scale


def tile_kernel(flip, reverse, sub, f0, f1, f2, f3, moving, norms, scales, before, lists, tile, row, col, inner, words, cols):
    me = sub[0]
    feats = moving[:ROWS, :].astype(jnp.float32)
    half_norm = 0.5 * jnp.sum(feats * feats, axis=1, keepdims=True)

    if reverse:
        digits = moving[ROWS + reverse - NNB : ROWS + reverse, :].astype(jnp.float32).astype(jnp.int32)
        position = digits[:, :ROWS] * 64 + digits[:, ROWS:]
        group = position >> 7
        slice_at = (group * 11) >> 5
        group = (slice_at ^ me) * 3 + group - 3 * slice_at
        pieces = [(position & 127).astype(jnp.float32), jnp.left_shift(1, group).astype(jnp.float32)]
        own_scale = moving[ROWS + 2 * NNB :, :ROWS].astype(jnp.float32)[0:1]
    else:
        pieces = [jnp.zeros((32, ROWS), jnp.float32)]
        own_scale = scales[:, pl.ds(pl.multiple_of(me * ROWS, 128), ROWS)]
    stacked = jnp.concatenate(
        pieces + [FOLDED / own_scale, jnp.zeros((95, ROWS), jnp.float32)], axis=0
    )
    turned = stacked.T
    move_scale = turned[:, 32:33]
    if reverse:
        sublane = lax.broadcasted_iota(jnp.int32, (128, ROWS), 0).astype(jnp.float32)
        word = jnp.zeros((128, ROWS), jnp.float32)
        for m in range(NNB):
            word = word + jnp.where(pieces[0][m : m + 1, :] == sublane, pieces[1][m : m + 1, :], 0.0)
        words[...] = word.T.astype(jnp.int32)

    row_at = lax.broadcasted_iota(jnp.int32, (8, ROWS), 0)
    for slot, ref in enumerate((f0, f1, f2, f3)):
        inner[slot] = lax.dot_general(moving[:ROWS, :], ref[...], NT, preferred_element_type=jnp.float32)
        start = pl.multiple_of((me ^ slot) * ROWS, 128)
        listed = lists[0, :, pl.ds(start, ROWS)] - (me ^ flip) * ROWS
        inside = (listed >= 0) & (listed < ROWS)
        sublane = listed & 7
        bit = jnp.where(inside, listed >> 3, 0)
        first = jnp.where(inside & (bit < 24), jnp.left_shift(1, bit), 0)
        second = jnp.where(inside & (bit >= 24), jnp.left_shift(1, jnp.maximum(bit - 24, 0)), 0)
        low = jnp.zeros((8, ROWS), jnp.int32)
        high = jnp.zeros((8, ROWS), jnp.int32)
        for m in range(NNB):
            same = sublane[m : m + 1, :] == row_at
            low = low | jnp.where(same, first[m : m + 1, :], 0)
            high = high | jnp.where(same, second[m : m + 1, :], 0)
        norm = 0.5 * norms[slot : slot + 1, :]
        scale = 1.0 / scales[:, pl.ds(start, ROWS)]
        row_sum = jnp.zeros((8, ROWS), jnp.float32)
        step = 32
        for at in range(0, ROWS, step):
            source = low if at < 192 else high
            counts = [
                (source >> ((at // 8 + c) % 24)) & 1 for c in range(step // 8)
            ]
            count = jnp.concatenate(counts, axis=0)
            if reverse:
                word = words[at : at + step, :]
                count = count + jnp.concatenate(
                    [(word >> (3 * slot + g)) & 1 for g in range(3)], axis=1
                )
            power = inner[slot, at : at + step, :] - half_norm[at : at + step] - norm
            power = power * move_scale[at : at + step] * scale
            weight = jnp.exp2(power) * count.astype(jnp.float32)
            tile[at : at + step, slot * ROWS : (slot + 1) * ROWS] = weight.astype(jnp.bfloat16)
            for c in range(step // 8):
                row_sum = row_sum + weight[8 * c : 8 * c + 8, :]
            lanes = weight[:, 0:128] + weight[:, 128:256] + weight[:, 256:384]
            if slot == 0:
                cols[at : at + step, :] = lanes
            else:
                cols[at : at + step, :] = cols[at : at + step, :] + lanes
        total = jnp.sum(row_sum, axis=0, keepdims=True)
        row[slot : slot + 1, :] = before[slot : slot + 1, :] + total if reverse else total
    col[...] = jnp.sum(cols[...].T, axis=0, keepdims=True)


def col_kernel(x0, x1, far, t0, t1, t2, t3, t4, z0, z1, z2, z3, z4):
    block = jnp.concatenate([x0[...], x1[...], far[:EIG, :], far[EIG:, :]], axis=1)
    for tile, out in ((t1, z1), (t2, z2), (t3, z3), (t4, z4), (t0, z0)):
        out[...] = lax.dot_general(block, tile[...], NT, preferred_element_type=jnp.float32).astype(out.dtype)


def row_kernel(x0, x1, x2, x3, x4, t0, t1, t2, t3, t4, y0, y2, sent):
    for slot, out, at_out in ((1, sent, 0), (3, sent, EIG), (0, y0, 0), (2, y2, 0)):
        at = slot * ROWS
        total = jnp.zeros((EIG, ROWS), jnp.float32)
        for vectors, tile in ((x0, t0), (x1, t1), (x2, t2), (x3, t3), (x4, t4)):
            total = total + jnp.dot(
                vectors[...], tile[:, at : at + ROWS], preferred_element_type=jnp.float32
            )
        out[at_out : at_out + EIG, :] = total


def mix_kernel(own, root, y0, y1, y2, z0, z1, z2, z3, z4, mixed, gram):
    sides = y0[...] + y1[:EIG, :] + y2[...].astype(jnp.float32) + z0[...]
    for part in (z1, z2, z3, z4):
        sides = sides + part[...].astype(jnp.float32)
    inv = root[0:1, :]
    value = inv * (own[...] * inv + 0.5 * sides)
    mixed[...] = value
    total = lax.dot_general(
        value, value, NT, precision=lax.Precision.HIGHEST, preferred_element_type=jnp.float32
    )
    gram[...] = jnp.concatenate([total[: EIG // 2], total[EIG // 2 :]], axis=1)


def solve_kernel(factor, gram, mixed, out):
    rows = lax.broadcasted_iota(jnp.int32, (EIG, 2 * EIG), 0)
    lanes = lax.broadcasted_iota(jnp.int32, (EIG, 2 * EIG), 1)
    unit = (rows + EIG == lanes).astype(jnp.float32)
    square = jnp.concatenate([gram[:, :EIG], gram[:, EIG:]], axis=0)
    work = jnp.concatenate([square, jnp.zeros((EIG, EIG), jnp.float32)], axis=1) + unit
    done = []
    for at in range(0, EIG, 8):
        wide = [jnp.broadcast_to(work[:, at + j : at + j + 1], (EIG - at, 2 * EIG)) for j in range(8)]
        for j in range(8):
            root = lax.rsqrt(wide[j][j : j + 1, :])
            pivot = work[j : j + 1, :] * root
            done.append(pivot)
            lower = wide[j] * root
            work = work - lower * pivot
            for other in range(j + 1, 8):
                wide[other] = wide[other] - lower * (wide[other][j : j + 1, :] * root)
        work = work[8:]
    inverse = jnp.concatenate(done, axis=0)[:, EIG:]
    out[...] = factor * jnp.dot(
        inverse, mixed[...], precision=lax.Precision.HIGHEST, preferred_element_type=jnp.float32
    )


def local(features, scales, neighbor_lists, eigen_block):
    sub = lax.axis_index("sub").astype(jnp.int32)
    half = (neighbor_lists.shape[0] - 1) // 2
    total_rows = ROWS * lax.axis_size("blk") * lax.axis_size("sub")
    sub_arg = sub.reshape(1)

    block_scales = scales.astype(jnp.float32)[None, :]
    own_lists = lax.dynamic_slice_in_dim(neighbor_lists, sub * ROWS, ROWS, axis=2)
    first, second = call(
        functools.partial(pack_kernel, half),
        (bf16(ROWS + EXTRA, F),) * 2,
        specs=(SMEM, VMEM, VMEM, VMEM),
    )(sub_arg, features, block_scales, own_lists)

    first, second, ready, all_lists = lax.optimization_barrier(
        (first, second, features, neighbor_lists)
    )
    first = moved(first, *BAND[0])
    second = moved(second, *BAND[1])
    slot2 = moved(ready, 0, 2)
    slot1 = moved(ready, 0, 1)
    slot3 = moved(slot2, 0, 1)
    block = (features, slot1, slot2, slot3)

    tile_outs = (bf16(ROWS, SLOTS * ROWS), f32(SLOTS, ROWS), f32(1, ROWS))
    scratch = (
        pltpu.VMEM((SLOTS, ROWS, ROWS), jnp.float32),
        pltpu.VMEM((ROWS, 128), jnp.int32),
        pltpu.VMEM((ROWS, 128), jnp.float32),
    )

    def listed(d):
        return pl.BlockSpec((1, NNB, SLOTS * ROWS), lambda i: (half + d, 0, 0))

    def band_tile(index, moving, row, tokens=(), flops=1000):
        d, u = BAND[index]
        body = functools.partial(band_tile_kernel, u, NNB * (1 + index // 2))
        specs = (SMEM,) + (VMEM,) * 8 + (HBM,) * len(tokens) + (listed(d),)
        args = (sub_arg, *block, moving, norms, block_scales, row, *tokens, all_lists)
        tile, row, col = call(body, tile_outs, scratch, specs, flops)(*args)
        return tile, row, moved(col, -d, u)

    tile0, row, col0, norms = call(
        own_tile_kernel,
        tile_outs + (f32(SLOTS, ROWS),),
        scratch,
        (SMEM,) + (VMEM,) * 5 + (listed(0),),
    )(sub_arg, *block, block_scales, all_lists)
    first, second, row = lax.optimization_barrier((first, second, row))
    third = moved(first, *ONWARD[0])
    fourth = moved(second, *ONWARD[1])
    tile1, row, col1 = band_tile(0, first, row)
    tile2, row, col2 = band_tile(1, second, row)
    tile3, row, col3 = band_tile(2, third, row)
    tile4, row, col4 = band_tile(3, fourth, row, (col1, col2), 4 * 10**9)
    tiles = (tile0, tile1, tile2, tile3, tile4)

    pair = row[0:2] + moved(row[2:4], 0, 2)
    own = pair[0:1] + moved(pair[1:2], 0, 1)
    root = lax.rsqrt(1.0 + 0.5 * (own + col0 + col1 + col2 + col3 + col4))
    scaled_low = (eigen_block * root).astype(jnp.bfloat16)
    vectors = [moved(scaled_low, d, u) for d, u in BAND]
    x1 = moved(scaled_low, 0, 1)
    far = moved(jnp.concatenate([scaled_low, x1], axis=0), 0, 2)

    z_outs = (f32(EIG, ROWS),) + (bf16(EIG, ROWS),) * 4
    z0, z1, z2, z3, z4 = call(col_kernel, z_outs)(scaled_low, x1, far, *tiles)
    back = [moved(part, -d, u) for (d, u), part in zip(BAND, (z1, z2, z3, z4))]
    vectors, _ = lax.optimization_barrier((vectors, z0))
    y_outs = (f32(EIG, ROWS), f32(EIG, ROWS), f32(2 * EIG, ROWS))
    y0, y2, sent = call(row_kernel, y_outs)(scaled_low, *vectors, *tiles)
    other = moved(sent, 0, 1)
    across = moved((y2 + other[EIG:]).astype(jnp.bfloat16), 0, 2)
    mixed, gram = call(mix_kernel, (f32(EIG, ROWS), f32(EIG // 2, 2 * EIG)))(
        eigen_block, root, y0, other, across, z0, *back
    )
    n_blk, n_sub = lax.axis_size("blk"), lax.axis_size("sub")
    for partners in ROUNDS:
        parts = [gram]
        for flip_blk, flip_sub in partners:
            pairs = [
                (b * n_sub + s, (b ^ flip_blk) * n_sub + (s ^ flip_sub))
                for b in range(n_blk)
                for s in range(n_sub)
            ]
            parts.append(lax.ppermute(gram, ("blk", "sub"), pairs))
        gram = functools.reduce(jnp.add, parts)
    body = functools.partial(solve_kernel, math.sqrt(total_rows))
    return call(body, f32(EIG, ROWS))(gram, mixed)


def solution(mesh):
    placed = (P(("blk", "sub"), None), P("blk"), P(None, None, "blk"), P(None, ("blk", "sub")))
    return jax.shard_map(
        local, mesh=mesh, in_specs=placed, out_specs=P(None, ("blk", "sub")), check_vma=False
    )
```

```python
import functools
import math

import jax
import jax.numpy as jnp
from jax import lax
from jax.experimental import pallas as pl
from jax.experimental.pallas import tpu as pltpu
from jax.sharding import PartitionSpec as P

F = 768
ROWS = 384
SLOTS = 4
EIG = 64
NNB = 16
BAND = ((1, 2), (-2, 0), (3, 2), (-4, 0))
ROUTES = ((BAND[2], BAND[3]), (BAND[0], BAND[1]))
ONWARD = ((2, 0), (-2, 0))
EXTRA = 3 * NNB
ROUNDS = (((0, 1),), ((0, 2), (1, 0), (1, 2)), ((2, 0), (4, 0), (6, 0)), ((8, 0), (16, 0), (24, 0)))
FOLDED = 2.0 * math.log2(math.e) / F
NT = (((1,), (1,)), ((), ()))
LIMIT = 24 * 1024 * 1024


def moved(value, blocks, flip):
    n_blk, n_sub = lax.axis_size("blk"), lax.axis_size("sub")
    pairs = [
        (b * n_sub + s, ((b + blocks) % n_blk) * n_sub + (s ^ flip))
        for b in range(n_blk)
        for s in range(n_sub)
    ]
    return lax.ppermute(value, ("blk", "sub"), pairs)


def routed(value, back=False):
    n_blk, n_sub = lax.axis_size("blk"), lax.axis_size("sub")
    outs = []
    for part, routes in zip(value, ROUTES):
        pairs = []
        for b in range(n_blk):
            for s in range(n_sub):
                d, flip = routes[s % 2]
                pairs.append((b * n_sub + s, ((b - d if back else b + d) % n_blk) * n_sub + (s ^ flip)))
        outs.append(lax.ppermute(part, ("blk", "sub"), pairs))
    return outs


VMEM = pl.BlockSpec(memory_space=pltpu.VMEM)
SMEM = pl.BlockSpec(memory_space=pltpu.SMEM)
HBM = pl.BlockSpec(memory_space=pltpu.HBM)


def call(body, outs, scratch=(), specs=None, flops=1000):
    def run(*args):
        return pl.pallas_call(
            body,
            grid=(1,),
            out_shape=outs,
            in_specs=list(specs) if specs else [VMEM] * len(args),
            out_specs=jax.tree.map(lambda _: VMEM, outs),
            scratch_shapes=list(scratch),
            compiler_params=pltpu.CompilerParams(vmem_limit_bytes=LIMIT),
            cost_estimate=pl.CostEstimate(flops=flops, bytes_accessed=1000, transcendentals=0),
        )(*args)

    return run


def f32(*shape):
    return jax.ShapeDtypeStruct(shape, jnp.float32)


def bf16(*shape):
    return jax.ShapeDtypeStruct(shape, jnp.bfloat16)


def own_tile_kernel(sub, f0, f1, f2, f3, scales, lists, tile, row, col, norms, inner, words, cols):
    ones = jnp.ones((8, F), jnp.bfloat16)
    for slot, ref in enumerate((f0, f1, f2, f3)):
        value = ref[...].astype(jnp.float32)
        square = value * value
        high = square.astype(jnp.bfloat16)
        low = (square - high.astype(jnp.float32)).astype(jnp.bfloat16)
        total = lax.dot_general(ones, high, NT, preferred_element_type=jnp.float32)
        total = total + lax.dot_general(ones, low, NT, preferred_element_type=jnp.float32)
        norms[slot : slot + 1, :] = total[0:1, :]
    tile_kernel(0, 0, sub, f0, f1, f2, f3, f0, norms, scales, None, lists, tile, row, col, inner, words, cols)


def band_tile_kernel(flip, reverse, sub, *refs):
    tile_kernel(flip, reverse, sub, *refs[:8], *refs[-7:])


def pack_kernel(half, sub, features, scales, lists, first, second):
    at = pl.multiple_of(sub[0] * ROWS, 128)
    scale = jnp.concatenate([scales[:, pl.ds(at, ROWS)], jnp.ones((1, ROWS), jnp.float32)], axis=1)
    scale = jnp.broadcast_to(scale, (NNB, 2 * ROWS)).astype(jnp.bfloat16)
    for out, chosen in ((first, BAND[0::2]), (second, BAND[1::2])):
        out[:ROWS, :] = features[...]
        for index, (d, _) in enumerate(chosen):
            position = lists[half - d]
            digits = jnp.concatenate([position >> 6, position & 63], axis=1)
            start = ROWS + NNB * index
            out[start : start + NNB, :] = digits.astype(jnp.float32).astype(jnp.bfloat16)
        out[ROWS + 2 * NNB :, :] = scale


def tile_kernel(flip, reverse, sub, f0, f1, f2, f3, moving, norms, scales, before, lists, tile, row, col, inner, words, cols):
    me = sub[0]
    feats = moving[:ROWS, :].astype(jnp.float32)
    half_norm = 0.5 * jnp.sum(feats * feats, axis=1, keepdims=True)

    if reverse:
        digits = moving[ROWS + reverse - NNB : ROWS + reverse, :].astype(jnp.float32).astype(jnp.int32)
        position = digits[:, :ROWS] * 64 + digits[:, ROWS:]
        group = position >> 7
        slice_at = (group * 11) >> 5
        group = (slice_at ^ me) * 3 + group - 3 * slice_at
        pieces = [(position & 127).astype(jnp.float32), jnp.left_shift(1, group).astype(jnp.float32)]
        own_scale = moving[ROWS + 2 * NNB :, :ROWS].astype(jnp.float32)[0:1]
    else:
        pieces = [jnp.zeros((32, ROWS), jnp.float32)]
        own_scale = scales[:, pl.ds(pl.multiple_of(me * ROWS, 128), ROWS)]
    stacked = jnp.concatenate(
        pieces + [FOLDED / own_scale, jnp.zeros((95, ROWS), jnp.float32)], axis=0
    )
    turned = stacked.T
    move_scale = turned[:, 32:33]
    if reverse:
        sublane = lax.broadcasted_iota(jnp.int32, (128, ROWS), 0).astype(jnp.float32)
        word = jnp.zeros((128, ROWS), jnp.float32)
        for m in range(NNB):
            word = word + jnp.where(pieces[0][m : m + 1, :] == sublane, pieces[1][m : m + 1, :], 0.0)
        words[...] = word.T.astype(jnp.int32)

    row_at = lax.broadcasted_iota(jnp.int32, (8, ROWS), 0)
    for slot, ref in enumerate((f0, f1, f2, f3)):
        inner[slot] = lax.dot_general(moving[:ROWS, :], ref[...], NT, preferred_element_type=jnp.float32)
        start = pl.multiple_of((me ^ slot) * ROWS, 128)
        listed = lists[0, :, pl.ds(start, ROWS)] - (me ^ flip) * ROWS
        inside = (listed >= 0) & (listed < ROWS)
        sublane = listed & 7
        bit = jnp.where(inside, listed >> 3, 0)
        first = jnp.where(inside & (bit < 24), jnp.left_shift(1, bit), 0)
        second = jnp.where(inside & (bit >= 24), jnp.left_shift(1, jnp.maximum(bit - 24, 0)), 0)
        low = jnp.zeros((8, ROWS), jnp.int32)
        high = jnp.zeros((8, ROWS), jnp.int32)
        for m in range(NNB):
            same = sublane[m : m + 1, :] == row_at
            low = low | jnp.where(same, first[m : m + 1, :], 0)
            high = high | jnp.where(same, second[m : m + 1, :], 0)
        norm = 0.5 * norms[slot : slot + 1, :]
        scale = 1.0 / scales[:, pl.ds(start, ROWS)]
        row_sum = jnp.zeros((8, ROWS), jnp.float32)
        step = 32
        for at in range(0, ROWS, step):
            source = low if at < 192 else high
            counts = [
                (source >> ((at // 8 + c) % 24)) & 1 for c in range(step // 8)
            ]
            count = jnp.concatenate(counts, axis=0)
            if reverse:
                word = words[at : at + step, :]
                count = count + jnp.concatenate(
                    [(word >> (3 * slot + g)) & 1 for g in range(3)], axis=1
                )
            power = inner[slot, at : at + step, :] - half_norm[at : at + step] - norm
            power = power * move_scale[at : at + step] * scale
            weight = jnp.exp2(power) * count.astype(jnp.float32)
            tile[at : at + step, slot * ROWS : (slot + 1) * ROWS] = weight.astype(jnp.bfloat16)
            for c in range(step // 8):
                row_sum = row_sum + weight[8 * c : 8 * c + 8, :]
            lanes = weight[:, 0:128] + weight[:, 128:256] + weight[:, 256:384]
            if slot == 0:
                cols[at : at + step, :] = lanes
            else:
                cols[at : at + step, :] = cols[at : at + step, :] + lanes
        total = jnp.sum(row_sum, axis=0, keepdims=True)
        row[slot : slot + 1, :] = before[slot : slot + 1, :] + total if reverse else total
    col[...] = jnp.sum(cols[...].T, axis=0, keepdims=True)


def col_kernel(sub, x0, x1, far, t0, t1, t2, t3, t4, z0, keep, give):
    block = jnp.concatenate([x0[...], x1[...], far[:EIG, :], far[EIG:, :]], axis=1)
    z1, z2, z3, z4 = [
        lax.dot_general(block, tile[...], NT, preferred_element_type=jnp.float32)
        for tile in (t1, t2, t3, t4)
    ]
    odd = sub[0] % 2 == 1
    for at, (even_one, odd_one) in ((0, (z3, z4)), (EIG, (z1, z2))):
        keep[at : at + EIG, :] = jnp.where(odd, odd_one, even_one).astype(jnp.bfloat16)
        give[at : at + EIG, :] = jnp.where(odd, even_one, odd_one).astype(jnp.bfloat16)
    z0[...] = lax.dot_general(block, t0[...], NT, preferred_element_type=jnp.float32)


def row_kernel(sub, x0, one, two, got, t0, t1, t2, t3, t4, kept, sent):
    odd = sub[0] % 2 == 1
    one_x, two_x = one[:EIG, :].astype(jnp.float32), two[:EIG, :].astype(jnp.float32)
    got_one, got_two = got[:EIG, :].astype(jnp.float32), got[EIG:, :].astype(jnp.float32)
    x1 = jnp.where(odd, got_two, two_x).astype(jnp.bfloat16)
    x2 = jnp.where(odd, two_x, got_two).astype(jnp.bfloat16)
    x3 = jnp.where(odd, got_one, one_x).astype(jnp.bfloat16)
    x4 = jnp.where(odd, one_x, got_one).astype(jnp.bfloat16)
    for half, out in ((1, sent), (0, kept)):
        at = half * 2 * ROWS
        total = jnp.zeros((EIG, 2 * ROWS), jnp.float32)
        for vectors, tile in ((x0[...], t0), (x1, t1), (x2, t2), (x3, t3), (x4, t4)):
            total = total + jnp.dot(
                vectors, tile[:, at : at + 2 * ROWS], preferred_element_type=jnp.float32
            )
        out[...] = total.astype(out.dtype)


def mix_kernel(own, root, kept, got, one, two, z0, swapped, mixed, gram):
    sides = kept[:, :ROWS] + got[:, :ROWS].astype(jnp.float32) + z0[...] + swapped[...]
    for part in (one, two):
        sides = sides + part[:EIG, :].astype(jnp.float32)
    inv = root[0:1, :]
    value = inv * (own[...] * inv + 0.5 * sides)
    mixed[...] = value
    total = lax.dot_general(
        value, value, NT, precision=lax.Precision.HIGHEST, preferred_element_type=jnp.float32
    )
    gram[...] = jnp.concatenate([total[: EIG // 2], total[EIG // 2 :]], axis=1)


def solve_kernel(factor, gram, mixed, out):
    rows = lax.broadcasted_iota(jnp.int32, (EIG, 2 * EIG), 0)
    lanes = lax.broadcasted_iota(jnp.int32, (EIG, 2 * EIG), 1)
    unit = (rows + EIG == lanes).astype(jnp.float32)
    square = jnp.concatenate([gram[:, :EIG], gram[:, EIG:]], axis=0)
    work = jnp.concatenate([square, jnp.zeros((EIG, EIG), jnp.float32)], axis=1) + unit
    done = []
    for at in range(0, EIG, 8):
        wide = [jnp.broadcast_to(work[:, at + j : at + j + 1], (EIG - at, 2 * EIG)) for j in range(8)]
        for j in range(8):
            root = lax.rsqrt(wide[j][j : j + 1, :])
            pivot = work[j : j + 1, :] * root
            done.append(pivot)
            lower = wide[j] * root
            work = work - lower * pivot
            for other in range(j + 1, 8):
                wide[other] = wide[other] - lower * (wide[other][j : j + 1, :] * root)
        work = work[8:]
    inverse = jnp.concatenate(done, axis=0)[:, EIG:]
    out[...] = factor * jnp.dot(
        inverse, mixed[...], precision=lax.Precision.HIGHEST, preferred_element_type=jnp.float32
    )


def local(features, scales, neighbor_lists, eigen_block):
    sub = lax.axis_index("sub").astype(jnp.int32)
    half = (neighbor_lists.shape[0] - 1) // 2
    total_rows = ROWS * lax.axis_size("blk") * lax.axis_size("sub")
    sub_arg = sub.reshape(1)

    block_scales = scales.astype(jnp.float32)[None, :]
    own_lists = lax.dynamic_slice_in_dim(neighbor_lists, sub * ROWS, ROWS, axis=2)
    first, second = call(
        functools.partial(pack_kernel, half),
        (bf16(ROWS + EXTRA, F),) * 2,
        specs=(SMEM, VMEM, VMEM, VMEM),
    )(sub_arg, features, block_scales, own_lists)

    first, second, ready, all_lists = lax.optimization_barrier(
        (first, second, features, neighbor_lists)
    )
    first = moved(first, *BAND[0])
    second = moved(second, *BAND[1])
    slot2 = moved(ready, 0, 2)
    slot1 = moved(ready, 0, 1)
    slot3 = moved(slot2, 0, 1)
    block = (features, slot1, slot2, slot3)

    tile_outs = (bf16(ROWS, SLOTS * ROWS), f32(SLOTS, ROWS), f32(1, ROWS))
    scratch = (
        pltpu.VMEM((SLOTS, ROWS, ROWS), jnp.float32),
        pltpu.VMEM((ROWS, 128), jnp.int32),
        pltpu.VMEM((ROWS, 128), jnp.float32),
    )

    def listed(d):
        return pl.BlockSpec((1, NNB, SLOTS * ROWS), lambda i: (half + d, 0, 0))

    def band_tile(index, moving, row, tokens=(), flops=1000):
        d, u = BAND[index]
        body = functools.partial(band_tile_kernel, u, NNB * (1 + index // 2))
        specs = (SMEM,) + (VMEM,) * 8 + (HBM,) * len(tokens) + (listed(d),)
        args = (sub_arg, *block, moving, norms, block_scales, row, *tokens, all_lists)
        tile, row, col = call(body, tile_outs, scratch, specs, flops)(*args)
        return tile, row, moved(col, -d, u)

    tile0, row, col0, norms = call(
        own_tile_kernel,
        tile_outs + (f32(SLOTS, ROWS),),
        scratch,
        (SMEM,) + (VMEM,) * 5 + (listed(0),),
    )(sub_arg, *block, block_scales, all_lists)
    first, second, row = lax.optimization_barrier((first, second, row))
    third = moved(first, *ONWARD[0])
    fourth = moved(second, *ONWARD[1])
    tile1, row, col1 = band_tile(0, first, row)
    tile2, row, col2 = band_tile(1, second, row)
    tile3, row, col3 = band_tile(2, third, row)
    tile4, row, col4 = band_tile(3, fourth, row, (col1, col2), 4 * 10**9)
    tiles = (tile0, tile1, tile2, tile3, tile4)

    pair = row[0:2] + moved(row[2:4], 0, 2)
    own = pair[0:1] + moved(pair[1:2], 0, 1)
    root = lax.rsqrt(1.0 + 0.5 * (own + col0 + col1 + col2 + col3 + col4))
    scaled_low = (eigen_block * root).astype(jnp.bfloat16)
    pair = jnp.concatenate([scaled_low, moved(scaled_low, 0, 1)], axis=0)
    one, two = routed((pair, pair))
    far = moved(pair, 0, 2)
    swapped = moved(jnp.concatenate([one[EIG:], two[EIG:]], axis=0), 0, 1)

    with_sub = (SMEM,) + (VMEM,) * 8
    z_outs = (f32(EIG, ROWS), bf16(2 * EIG, ROWS), bf16(2 * EIG, ROWS))
    z0, keep, give = call(col_kernel, z_outs, specs=with_sub)(
        sub_arg, scaled_low, pair[EIG:], far, *tiles
    )
    taken = moved(give, 0, 1)
    one_back, two_back = routed(
        (
            jnp.concatenate([keep[:EIG], taken[:EIG]], axis=0),
            jnp.concatenate([keep[EIG:], taken[EIG:]], axis=0),
        ),
        back=True,
    )
    swapped, _ = lax.optimization_barrier((swapped, z0))
    y_outs = (f32(EIG, 2 * ROWS), bf16(EIG, 2 * ROWS))
    kept, sent = call(row_kernel, y_outs, specs=with_sub + (VMEM,))(
        sub_arg, scaled_low, one, two, swapped, *tiles
    )
    got = moved(sent, 0, 2)
    owed = kept[:, ROWS:] + got[:, ROWS:].astype(jnp.float32)
    owed = owed + one_back[EIG:].astype(jnp.float32) + two_back[EIG:].astype(jnp.float32)
    mixed, gram = call(mix_kernel, (f32(EIG, ROWS), f32(EIG // 2, 2 * EIG)))(
        eigen_block, root, kept, got, one_back, two_back, z0, moved(owed, 0, 1)
    )
    n_blk, n_sub = lax.axis_size("blk"), lax.axis_size("sub")
    for partners in ROUNDS:
        parts = [gram]
        for flip_blk, flip_sub in partners:
            pairs = [
                (b * n_sub + s, (b ^ flip_blk) * n_sub + (s ^ flip_sub))
                for b in range(n_blk)
                for s in range(n_sub)
            ]
            parts.append(lax.ppermute(gram, ("blk", "sub"), pairs))
        gram = functools.reduce(jnp.add, parts)
    body = functools.partial(solve_kernel, math.sqrt(total_rows))
    return call(body, f32(EIG, ROWS))(gram, mixed)


def solution(mesh):
    placed = (P(("blk", "sub"), None), P("blk"), P(None, None, "blk"), P(None, ("blk", "sub")))
    return jax.shard_map(
        local, mesh=mesh, in_specs=placed, out_specs=P(None, ("blk", "sub")), check_vma=False
    )
```

```python
import functools
import math

import jax
import jax.numpy as jnp
from jax import lax
from jax.experimental import pallas as pl
from jax.experimental.pallas import tpu as pltpu
from jax.sharding import PartitionSpec as P

F = 768
ROWS = 384
SLOTS = 4
EIG = 64
NNB = 16
BAND = ((-2, 0), (1, 2), (-4, 0), (3, 2))
ROUTES = ((BAND[2], BAND[3]), (BAND[0], BAND[1]))
ONWARD = ((-2, 0), (2, 0))
EXTRA = 2 * NNB
ROUNDS = (((0, 1),), ((0, 2), (1, 0), (1, 2)), ((2, 0), (4, 0), (6, 0)), ((8, 0), (16, 0), (24, 0)))
FOLDED = 2.0 * math.log2(math.e) / F
NT = (((1,), (1,)), ((), ()))
LIMIT = 24 * 1024 * 1024


def moved(value, blocks, flip):
    n_blk, n_sub = lax.axis_size("blk"), lax.axis_size("sub")
    pairs = [
        (b * n_sub + s, ((b + blocks) % n_blk) * n_sub + (s ^ flip))
        for b in range(n_blk)
        for s in range(n_sub)
    ]
    return lax.ppermute(value, ("blk", "sub"), pairs)


def routed(value, back=False):
    n_blk, n_sub = lax.axis_size("blk"), lax.axis_size("sub")
    outs = []
    for part, routes in zip(value, ROUTES):
        pairs = []
        for b in range(n_blk):
            for s in range(n_sub):
                d, flip = routes[s % 2]
                pairs.append((b * n_sub + s, ((b - d if back else b + d) % n_blk) * n_sub + (s ^ flip)))
        outs.append(lax.ppermute(part, ("blk", "sub"), pairs))
    return outs


VMEM = pl.BlockSpec(memory_space=pltpu.VMEM)
SMEM = pl.BlockSpec(memory_space=pltpu.SMEM)
HBM = pl.BlockSpec(memory_space=pltpu.HBM)


def call(body, outs, scratch=(), specs=None, flops=1000):
    def run(*args):
        return pl.pallas_call(
            body,
            grid=(1,),
            out_shape=outs,
            in_specs=list(specs) if specs else [VMEM] * len(args),
            out_specs=jax.tree.map(lambda _: VMEM, outs),
            scratch_shapes=list(scratch),
            compiler_params=pltpu.CompilerParams(vmem_limit_bytes=LIMIT),
            cost_estimate=pl.CostEstimate(flops=flops, bytes_accessed=1000, transcendentals=0),
        )(*args)

    return run


def f32(*shape):
    return jax.ShapeDtypeStruct(shape, jnp.float32)


def bf16(*shape):
    return jax.ShapeDtypeStruct(shape, jnp.bfloat16)


def own_tile_kernel(sub, f0, f1, f2, f3, scales, lists, tile, row, col, norms, inner, words, cols):
    ones = jnp.ones((8, F), jnp.bfloat16)
    for slot, ref in enumerate((f0, f1, f2, f3)):
        value = ref[...].astype(jnp.float32)
        square = value * value
        high = square.astype(jnp.bfloat16)
        low = (square - high.astype(jnp.float32)).astype(jnp.bfloat16)
        total = lax.dot_general(ones, high, NT, preferred_element_type=jnp.float32)
        total = total + lax.dot_general(ones, low, NT, preferred_element_type=jnp.float32)
        norms[slot : slot + 1, :] = total[0:1, :]
    tile_kernel(0, 0, sub, f0, f1, f2, f3, f0, norms, scales, None, lists, tile, row, col, inner, words, cols)


def band_tile_kernel(flip, reverse, sub, *refs):
    tile_kernel(flip, reverse, sub, *refs[:8], *refs[-7:])


def pack_kernel(half, sub, features, scales, lists, first, second):
    at = pl.multiple_of(sub[0] * ROWS, 128)
    scale = jnp.concatenate([scales[:, pl.ds(at, ROWS)], jnp.ones((1, ROWS), jnp.float32)], axis=1)
    scale = jnp.broadcast_to(scale, (NNB, 2 * ROWS)).astype(jnp.bfloat16)
    for out, chosen in ((first, BAND[0::2]), (second, BAND[1::2])):
        out[:ROWS, :] = features[...]
        position = jnp.concatenate([lists[half - d] for d, _ in chosen], axis=1)
        group = position >> 7
        code = jnp.left_shift(128 + (position & 127), group & 7)
        code = jnp.where(group >= 8, -code, code)
        out[ROWS : ROWS + NNB, :] = code.astype(jnp.float32).astype(jnp.bfloat16)
        out[ROWS + NNB :, :] = scale


def tile_kernel(flip, reverse, sub, f0, f1, f2, f3, moving, norms, scales, before, lists, tile, row, col, inner, words, cols):
    me = sub[0]
    feats = moving[:ROWS, :].astype(jnp.float32)
    half_norm = 0.5 * jnp.sum(feats * feats, axis=1, keepdims=True)

    if reverse:
        code = moving[ROWS : ROWS + NNB, (reverse - 1) * ROWS : reverse * ROWS].astype(jnp.float32)
        code = code.astype(jnp.int32)
        size = jnp.abs(code)
        power = jnp.zeros_like(size)
        for bit in range(1, 8):
            power = power + (size >= (128 << bit)).astype(jnp.int32)
        lane = (size >> power) - 128
        group = power + jnp.where(code < 0, 8, 0)
        slice_at = (group * 11) >> 5
        group = (slice_at ^ me) * 3 + group - 3 * slice_at
        pieces = [lane.astype(jnp.float32), jnp.left_shift(1, group).astype(jnp.float32)]
        own_scale = moving[ROWS + NNB :, :ROWS].astype(jnp.float32)[0:1]
    else:
        pieces = [jnp.zeros((32, ROWS), jnp.float32)]
        own_scale = scales[:, pl.ds(pl.multiple_of(me * ROWS, 128), ROWS)]
    stacked = jnp.concatenate(
        pieces + [FOLDED / own_scale, jnp.zeros((95, ROWS), jnp.float32)], axis=0
    )
    turned = stacked.T
    move_scale = turned[:, 32:33]
    if reverse:
        sublane = lax.broadcasted_iota(jnp.int32, (128, ROWS), 0).astype(jnp.float32)
        word = jnp.zeros((128, ROWS), jnp.float32)
        for m in range(NNB):
            word = word + jnp.where(pieces[0][m : m + 1, :] == sublane, pieces[1][m : m + 1, :], 0.0)
        words[...] = word.T.astype(jnp.int32)

    row_at = lax.broadcasted_iota(jnp.int32, (8, ROWS), 0)
    for slot, ref in enumerate((f0, f1, f2, f3)):
        inner[slot] = lax.dot_general(moving[:ROWS, :], ref[...], NT, preferred_element_type=jnp.float32)
        start = pl.multiple_of((me ^ slot) * ROWS, 128)
        listed = lists[0, :, pl.ds(start, ROWS)] - (me ^ flip) * ROWS
        inside = (listed >= 0) & (listed < ROWS)
        sublane = listed & 7
        bit = jnp.where(inside, listed >> 3, 0)
        first = jnp.where(inside & (bit < 24), jnp.left_shift(1, bit), 0)
        second = jnp.where(inside & (bit >= 24), jnp.left_shift(1, jnp.maximum(bit - 24, 0)), 0)
        low = jnp.zeros((8, ROWS), jnp.int32)
        high = jnp.zeros((8, ROWS), jnp.int32)
        for m in range(NNB):
            same = sublane[m : m + 1, :] == row_at
            low = low | jnp.where(same, first[m : m + 1, :], 0)
            high = high | jnp.where(same, second[m : m + 1, :], 0)
        norm = 0.5 * norms[slot : slot + 1, :]
        scale = 1.0 / scales[:, pl.ds(start, ROWS)]
        row_sum = jnp.zeros((8, ROWS), jnp.float32)
        step = 32
        for at in range(0, ROWS, step):
            source = low if at < 192 else high
            counts = [
                (source >> ((at // 8 + c) % 24)) & 1 for c in range(step // 8)
            ]
            count = jnp.concatenate(counts, axis=0)
            if reverse:
                word = words[at : at + step, :]
                count = count + jnp.concatenate(
                    [(word >> (3 * slot + g)) & 1 for g in range(3)], axis=1
                )
            power = inner[slot, at : at + step, :] - half_norm[at : at + step] - norm
            power = power * move_scale[at : at + step] * scale
            weight = jnp.exp2(power) * count.astype(jnp.float32)
            tile[at : at + step, slot * ROWS : (slot + 1) * ROWS] = weight.astype(jnp.bfloat16)
            for c in range(step // 8):
                row_sum = row_sum + weight[8 * c : 8 * c + 8, :]
            lanes = weight[:, 0:128] + weight[:, 128:256] + weight[:, 256:384]
            if slot == 0:
                cols[at : at + step, :] = lanes
            else:
                cols[at : at + step, :] = cols[at : at + step, :] + lanes
        total = jnp.sum(row_sum, axis=0, keepdims=True)
        row[slot : slot + 1, :] = before[slot : slot + 1, :] + total if reverse else total
    col[...] = jnp.sum(cols[...].T, axis=0, keepdims=True)


def col_kernel(sub, x0, x1, far, t0, t1, t2, t3, t4, z0, keep, give):
    block = jnp.concatenate([x0[...], x1[...], far[:EIG, :], far[EIG:, :]], axis=1)
    z1, z2, z3, z4 = [
        lax.dot_general(block, tile[...], NT, preferred_element_type=jnp.float32)
        for tile in (t1, t2, t3, t4)
    ]
    odd = sub[0] % 2 == 1
    for at, (even_one, odd_one) in ((0, (z3, z4)), (EIG, (z1, z2))):
        keep[at : at + EIG, :] = jnp.where(odd, odd_one, even_one).astype(jnp.bfloat16)
        give[at : at + EIG, :] = jnp.where(odd, even_one, odd_one).astype(jnp.bfloat16)
    z0[...] = lax.dot_general(block, t0[...], NT, preferred_element_type=jnp.float32)


def row_kernel(sub, x0, one, two, got, t0, t1, t2, t3, t4, kept, sent):
    odd = sub[0] % 2 == 1
    one_x, two_x = one[:EIG, :].astype(jnp.float32), two[:EIG, :].astype(jnp.float32)
    got_one, got_two = got[:EIG, :].astype(jnp.float32), got[EIG:, :].astype(jnp.float32)
    x1 = jnp.where(odd, got_two, two_x).astype(jnp.bfloat16)
    x2 = jnp.where(odd, two_x, got_two).astype(jnp.bfloat16)
    x3 = jnp.where(odd, got_one, one_x).astype(jnp.bfloat16)
    x4 = jnp.where(odd, one_x, got_one).astype(jnp.bfloat16)
    for half, out in ((1, sent), (0, kept)):
        at = half * 2 * ROWS
        total = jnp.zeros((EIG, 2 * ROWS), jnp.float32)
        for vectors, tile in ((x0[...], t0), (x1, t1), (x2, t2), (x3, t3), (x4, t4)):
            total = total + jnp.dot(
                vectors, tile[:, at : at + 2 * ROWS], preferred_element_type=jnp.float32
            )
        out[...] = total.astype(out.dtype)


def mix_kernel(own, root, kept, got, one, two, z0, swapped, mixed, gram):
    sides = kept[:, :ROWS] + got[:, :ROWS].astype(jnp.float32) + z0[...] + swapped[...]
    for part in (one, two):
        sides = sides + part[:EIG, :].astype(jnp.float32)
    inv = root[0:1, :]
    value = inv * (own[...] * inv + 0.5 * sides)
    mixed[...] = value
    total = lax.dot_general(
        value, value, NT, precision=lax.Precision.HIGHEST, preferred_element_type=jnp.float32
    )
    gram[...] = jnp.concatenate([total[: EIG // 2], total[EIG // 2 :]], axis=1)


def solve_kernel(factor, gram, mixed, out):
    rows = lax.broadcasted_iota(jnp.int32, (EIG, 2 * EIG), 0)
    lanes = lax.broadcasted_iota(jnp.int32, (EIG, 2 * EIG), 1)
    unit = (rows + EIG == lanes).astype(jnp.float32)
    square = jnp.concatenate([gram[:, :EIG], gram[:, EIG:]], axis=0)
    work = jnp.concatenate([square, jnp.zeros((EIG, EIG), jnp.float32)], axis=1) + unit
    done = []
    for at in range(0, EIG, 8):
        wide = [jnp.broadcast_to(work[:, at + j : at + j + 1], (EIG - at, 2 * EIG)) for j in range(8)]
        for j in range(8):
            root = lax.rsqrt(wide[j][j : j + 1, :])
            pivot = work[j : j + 1, :] * root
            done.append(pivot)
            lower = wide[j] * root
            work = work - lower * pivot
            for other in range(j + 1, 8):
                wide[other] = wide[other] - lower * (wide[other][j : j + 1, :] * root)
        work = work[8:]
    inverse = jnp.concatenate(done, axis=0)[:, EIG:]
    out[...] = factor * jnp.dot(
        inverse, mixed[...], precision=lax.Precision.HIGHEST, preferred_element_type=jnp.float32
    )


def local(features, scales, neighbor_lists, eigen_block):
    sub = lax.axis_index("sub").astype(jnp.int32)
    half = (neighbor_lists.shape[0] - 1) // 2
    total_rows = ROWS * lax.axis_size("blk") * lax.axis_size("sub")
    sub_arg = sub.reshape(1)

    block_scales = scales.astype(jnp.float32)[None, :]
    own_lists = lax.dynamic_slice_in_dim(neighbor_lists, sub * ROWS, ROWS, axis=2)
    first, second = call(
        functools.partial(pack_kernel, half),
        (bf16(ROWS + EXTRA, F),) * 2,
        specs=(SMEM, VMEM, VMEM, VMEM),
    )(sub_arg, features, block_scales, own_lists)

    first, second, ready, all_lists = lax.optimization_barrier(
        (first, second, features, neighbor_lists)
    )
    first = moved(first, *BAND[0])
    second = moved(second, *BAND[1])
    slot2 = moved(ready, 0, 2)
    slot1 = moved(ready, 0, 1)
    slot3 = moved(slot2, 0, 1)
    block = (features, slot1, slot2, slot3)

    tile_outs = (bf16(ROWS, SLOTS * ROWS), f32(SLOTS, ROWS), f32(1, ROWS))
    scratch = (
        pltpu.VMEM((SLOTS, ROWS, ROWS), jnp.float32),
        pltpu.VMEM((ROWS, 128), jnp.int32),
        pltpu.VMEM((ROWS, 128), jnp.float32),
    )

    def listed(d):
        return pl.BlockSpec((1, NNB, SLOTS * ROWS), lambda i: (half + d, 0, 0))

    def band_tile(index, moving, row, tokens=(), flops=1000):
        d, u = BAND[index]
        body = functools.partial(band_tile_kernel, u, 1 + index // 2)
        specs = (SMEM,) + (VMEM,) * 8 + (HBM,) * len(tokens) + (listed(d),)
        args = (sub_arg, *block, moving, norms, block_scales, row, *tokens, all_lists)
        tile, row, col = call(body, tile_outs, scratch, specs, flops)(*args)
        return tile, row, moved(col, -d, u)

    tile0, row, col0, norms = call(
        own_tile_kernel,
        tile_outs + (f32(SLOTS, ROWS),),
        scratch,
        (SMEM,) + (VMEM,) * 5 + (listed(0),),
    )(sub_arg, *block, block_scales, all_lists)
    first, second, row = lax.optimization_barrier((first, second, row))
    third = moved(first, *ONWARD[0])
    fourth = moved(second, *ONWARD[1])
    tile1, row, col1 = band_tile(0, first, row)
    tile2, row, col2 = band_tile(1, second, row)
    tile3, row, col3 = band_tile(2, third, row)
    tile4, row, col4 = band_tile(3, fourth, row, (col1, col2), 4 * 10**9)
    tiles = (tile0, tile1, tile2, tile3, tile4)

    pair = row[0:2] + moved(row[2:4], 0, 2)
    own = pair[0:1] + moved(pair[1:2], 0, 1)
    root = lax.rsqrt(1.0 + 0.5 * (own + col0 + col1 + col2 + col3 + col4))
    scaled_low = (eigen_block * root).astype(jnp.bfloat16)
    pair = jnp.concatenate([scaled_low, moved(scaled_low, 0, 1)], axis=0)
    one, two = routed((pair, pair))
    far = moved(pair, 0, 2)
    swapped = moved(jnp.concatenate([one[EIG:], two[EIG:]], axis=0), 0, 1)

    with_sub = (SMEM,) + (VMEM,) * 8
    z_outs = (f32(EIG, ROWS), bf16(2 * EIG, ROWS), bf16(2 * EIG, ROWS))
    z0, keep, give = call(col_kernel, z_outs, specs=with_sub)(
        sub_arg, scaled_low, pair[EIG:], far, *tiles
    )
    taken = moved(give, 0, 1)
    one_back, two_back = routed(
        (
            jnp.concatenate([keep[:EIG], taken[:EIG]], axis=0),
            jnp.concatenate([keep[EIG:], taken[EIG:]], axis=0),
        ),
        back=True,
    )
    swapped, _ = lax.optimization_barrier((swapped, z0))
    y_outs = (f32(EIG, 2 * ROWS), bf16(EIG, 2 * ROWS))
    kept, sent = call(row_kernel, y_outs, specs=with_sub + (VMEM,))(
        sub_arg, scaled_low, one, two, swapped, *tiles
    )
    got = moved(sent, 0, 2)
    owed = kept[:, ROWS:] + got[:, ROWS:].astype(jnp.float32)
    owed = owed + one_back[EIG:].astype(jnp.float32) + two_back[EIG:].astype(jnp.float32)
    mixed, gram = call(mix_kernel, (f32(EIG, ROWS), f32(EIG // 2, 2 * EIG)))(
        eigen_block, root, kept, got, one_back, two_back, z0, moved(owed, 0, 1)
    )
    n_blk, n_sub = lax.axis_size("blk"), lax.axis_size("sub")
    for partners in ROUNDS:
        parts = [gram]
        for flip_blk, flip_sub in partners:
            pairs = [
                (b * n_sub + s, (b ^ flip_blk) * n_sub + (s ^ flip_sub))
                for b in range(n_blk)
                for s in range(n_sub)
            ]
            parts.append(lax.ppermute(gram, ("blk", "sub"), pairs))
        gram = functools.reduce(jnp.add, parts)
    body = functools.partial(solve_kernel, math.sqrt(total_rows))
    return call(body, f32(EIG, ROWS))(gram, mixed)


def solution(mesh):
    placed = (P(("blk", "sub"), None), P("blk"), P(None, None, "blk"), P(None, ("blk", "sub")))
    return jax.shard_map(
        local, mesh=mesh, in_specs=placed, out_specs=P(None, ("blk", "sub")), check_vma=False
    )
```

```python
import functools
import math

import jax
import jax.numpy as jnp
from jax import lax
from jax.experimental import pallas as pl
from jax.experimental.pallas import tpu as pltpu
from jax.sharding import PartitionSpec as P

F = 768
ROWS = 384
SLOTS = 4
EIG = 64
NNB = 16
BAND = ((2, 0), (-1, 2), (4, 0), (-3, 2))
ROUTES = ((BAND[2], BAND[3]), (BAND[0], BAND[1]))
ONWARD = ((2, 0), (-2, 0))
EXTRA = 2 * NNB
ROUNDS = (((0, 1),), ((0, 2), (1, 0), (1, 2)), ((2, 0), (4, 0), (6, 0)), ((8, 0), (16, 0), (24, 0)))
FOLDED = 2.0 * math.log2(math.e) / F
NT = (((1,), (1,)), ((), ()))
LIMIT = 24 * 1024 * 1024


def moved(value, blocks, flip):
    n_blk, n_sub = lax.axis_size("blk"), lax.axis_size("sub")
    pairs = [
        (b * n_sub + s, ((b + blocks) % n_blk) * n_sub + (s ^ flip))
        for b in range(n_blk)
        for s in range(n_sub)
    ]
    return lax.ppermute(value, ("blk", "sub"), pairs)


def routed(value, back=False):
    n_blk, n_sub = lax.axis_size("blk"), lax.axis_size("sub")
    outs = []
    for part, routes in zip(value, ROUTES):
        pairs = []
        for b in range(n_blk):
            for s in range(n_sub):
                d, flip = routes[s % 2]
                pairs.append((b * n_sub + s, ((b - d if back else b + d) % n_blk) * n_sub + (s ^ flip)))
        outs.append(lax.ppermute(part, ("blk", "sub"), pairs))
    return outs


VMEM = pl.BlockSpec(memory_space=pltpu.VMEM)
SMEM = pl.BlockSpec(memory_space=pltpu.SMEM)
HBM = pl.BlockSpec(memory_space=pltpu.HBM)


def call(body, outs, scratch=(), specs=None, flops=1000):
    def run(*args):
        return pl.pallas_call(
            body,
            grid=(1,),
            out_shape=outs,
            in_specs=list(specs) if specs else [VMEM] * len(args),
            out_specs=jax.tree.map(lambda _: VMEM, outs),
            scratch_shapes=list(scratch),
            compiler_params=pltpu.CompilerParams(vmem_limit_bytes=LIMIT),
            cost_estimate=pl.CostEstimate(flops=flops, bytes_accessed=1000, transcendentals=0),
        )(*args)

    return run


def f32(*shape):
    return jax.ShapeDtypeStruct(shape, jnp.float32)


def bf16(*shape):
    return jax.ShapeDtypeStruct(shape, jnp.bfloat16)


def own_tile_kernel(sub, f0, f1, f2, f3, scales, lists, tile, row, col, norms, inner, words, cols):
    ones = jnp.ones((8, F), jnp.bfloat16)
    for slot, ref in enumerate((f0, f1, f2, f3)):
        value = ref[...].astype(jnp.float32)
        square = value * value
        high = square.astype(jnp.bfloat16)
        low = (square - high.astype(jnp.float32)).astype(jnp.bfloat16)
        total = lax.dot_general(ones, high, NT, preferred_element_type=jnp.float32)
        total = total + lax.dot_general(ones, low, NT, preferred_element_type=jnp.float32)
        norms[slot : slot + 1, :] = total[0:1, :]
    tile_kernel(0, 0, sub, f0, f1, f2, f3, f0, norms, scales, None, lists, tile, row, col, inner, words, cols)


def band_tile_kernel(flip, reverse, sub, *refs):
    tile_kernel(flip, reverse, sub, *refs[:8], *refs[-7:])


def pack_kernel(half, sub, features, scales, lists, first, second):
    at = pl.multiple_of(sub[0] * ROWS, 128)
    scale = jnp.concatenate([scales[pl.ds(at, ROWS)].reshape(1, ROWS), jnp.ones((1, ROWS), jnp.float32)], axis=1)
    scale = jnp.broadcast_to(scale, (NNB, 2 * ROWS)).astype(jnp.bfloat16)
    for out, chosen in ((first, BAND[0::2]), (second, BAND[1::2])):
        out[:ROWS, :] = features[...]
        position = jnp.concatenate([lists[half - d] for d, _ in chosen], axis=1)
        group = position >> 7
        code = jnp.left_shift(128 + (position & 127), group & 7)
        code = jnp.where(group >= 8, -code, code)
        out[ROWS : ROWS + NNB, :] = code.astype(jnp.float32).astype(jnp.bfloat16)
        out[ROWS + NNB :, :] = scale


def tile_kernel(flip, reverse, sub, f0, f1, f2, f3, moving, norms, scales, before, lists, tile, row, col, inner, words, cols):
    me = sub[0]
    feats = moving[:ROWS, :].astype(jnp.float32)
    half_norm = 0.5 * jnp.sum(feats * feats, axis=1, keepdims=True)

    if reverse:
        code = moving[ROWS : ROWS + NNB, (reverse - 1) * ROWS : reverse * ROWS].astype(jnp.float32)
        code = code.astype(jnp.int32)
        size = jnp.abs(code)
        power = jnp.zeros_like(size)
        for bit in range(1, 8):
            power = power + (size >= (128 << bit)).astype(jnp.int32)
        lane = (size >> power) - 128
        group = power + jnp.where(code < 0, 8, 0)
        slice_at = (group * 11) >> 5
        group = (slice_at ^ me) * 3 + group - 3 * slice_at
        pieces = [lane.astype(jnp.float32), jnp.left_shift(1, group).astype(jnp.float32)]
        own_scale = moving[ROWS + NNB :, :ROWS].astype(jnp.float32)[0:1]
    else:
        pieces = [jnp.zeros((32, ROWS), jnp.float32)]
        own_scale = scales[pl.ds(pl.multiple_of(me * ROWS, 128), ROWS)].reshape(1, ROWS)
    stacked = jnp.concatenate(
        pieces + [FOLDED / own_scale, jnp.zeros((95, ROWS), jnp.float32)], axis=0
    )
    turned = stacked.T
    move_scale = turned[:, 32:33]
    if reverse:
        sublane = lax.broadcasted_iota(jnp.int32, (128, ROWS), 0).astype(jnp.float32)
        word = jnp.zeros((128, ROWS), jnp.float32)
        for m in range(NNB):
            word = word + jnp.where(pieces[0][m : m + 1, :] == sublane, pieces[1][m : m + 1, :], 0.0)
        words[...] = word.T.astype(jnp.int32)

    row_at = lax.broadcasted_iota(jnp.int32, (8, ROWS), 0)
    for slot, ref in enumerate((f0, f1, f2, f3)):
        inner[slot] = lax.dot_general(moving[:ROWS, :], ref[...], NT, preferred_element_type=jnp.float32)
        start = pl.multiple_of((me ^ slot) * ROWS, 128)
        listed = lists[0, :, pl.ds(start, ROWS)] - (me ^ flip) * ROWS
        inside = (listed >= 0) & (listed < ROWS)
        sublane = listed & 7
        bit = jnp.where(inside, listed >> 3, 0)
        first = jnp.where(inside & (bit < 24), jnp.left_shift(1, bit), 0)
        second = jnp.where(inside & (bit >= 24), jnp.left_shift(1, jnp.maximum(bit - 24, 0)), 0)
        low = jnp.zeros((8, ROWS), jnp.int32)
        high = jnp.zeros((8, ROWS), jnp.int32)
        for m in range(NNB):
            same = sublane[m : m + 1, :] == row_at
            low = low | jnp.where(same, first[m : m + 1, :], 0)
            high = high | jnp.where(same, second[m : m + 1, :], 0)
        norm = 0.5 * norms[slot : slot + 1, :]
        scale = 1.0 / scales[pl.ds(start, ROWS)].reshape(1, ROWS)
        row_sum = jnp.zeros((8, ROWS), jnp.float32)
        step = 32
        for at in range(0, ROWS, step):
            source = low if at < 192 else high
            counts = [
                (source >> ((at // 8 + c) % 24)) & 1 for c in range(step // 8)
            ]
            count = jnp.concatenate(counts, axis=0)
            if reverse:
                word = words[at : at + step, :]
                count = count + jnp.concatenate(
                    [(word >> (3 * slot + g)) & 1 for g in range(3)], axis=1
                )
            power = inner[slot, at : at + step, :] - half_norm[at : at + step] - norm
            power = power * move_scale[at : at + step] * scale
            weight = jnp.exp2(power) * count.astype(jnp.float32)
            tile[at : at + step, slot * ROWS : (slot + 1) * ROWS] = weight.astype(jnp.bfloat16)
            for c in range(step // 8):
                row_sum = row_sum + weight[8 * c : 8 * c + 8, :]
            lanes = weight[:, 0:128] + weight[:, 128:256] + weight[:, 256:384]
            if slot == 0:
                cols[at : at + step, :] = lanes
            else:
                cols[at : at + step, :] = cols[at : at + step, :] + lanes
        total = jnp.sum(row_sum, axis=0, keepdims=True)
        row[slot : slot + 1, :] = before[slot : slot + 1, :] + total if reverse else total
    col[...] = jnp.sum(cols[...].T, axis=0, keepdims=True)


def col_kernel(sub, x0, x1, far, t0, t1, t2, t3, t4, z0, keep, give):
    block = jnp.concatenate([x0[...], x1[...], far[:EIG, :], far[EIG:, :]], axis=1)
    z1, z2, z3, z4 = [
        lax.dot_general(block, tile[...], NT, preferred_element_type=jnp.float32)
        for tile in (t1, t2, t3, t4)
    ]
    odd = sub[0] % 2 == 1
    for at, (even_one, odd_one) in ((0, (z3, z4)), (EIG, (z1, z2))):
        keep[at : at + EIG, :] = jnp.where(odd, odd_one, even_one).astype(jnp.bfloat16)
        give[at : at + EIG, :] = jnp.where(odd, even_one, odd_one).astype(jnp.bfloat16)
    z0[...] = lax.dot_general(block, t0[...], NT, preferred_element_type=jnp.float32)


def row_kernel(sub, x0, one, two, got, t0, t1, t2, t3, t4, kept, sent):
    odd = sub[0] % 2 == 1
    one_x, two_x = one[:EIG, :].astype(jnp.float32), two[:EIG, :].astype(jnp.float32)
    got_one, got_two = got[:EIG, :].astype(jnp.float32), got[EIG:, :].astype(jnp.float32)
    x1 = jnp.where(odd, got_two, two_x).astype(jnp.bfloat16)
    x2 = jnp.where(odd, two_x, got_two).astype(jnp.bfloat16)
    x3 = jnp.where(odd, got_one, one_x).astype(jnp.bfloat16)
    x4 = jnp.where(odd, one_x, got_one).astype(jnp.bfloat16)
    for half, out in ((1, sent), (0, kept)):
        at = half * 2 * ROWS
        total = jnp.zeros((EIG, 2 * ROWS), jnp.float32)
        for vectors, tile in ((x0[...], t0), (x1, t1), (x2, t2), (x3, t3), (x4, t4)):
            total = total + jnp.dot(
                vectors, tile[:, at : at + 2 * ROWS], preferred_element_type=jnp.float32
            )
        out[...] = total.astype(out.dtype)


def mix_kernel(own, root, kept, got, one, two, z0, swapped, mixed, gram):
    sides = kept[:, :ROWS] + got[:, :ROWS].astype(jnp.float32) + z0[...] + swapped[...]
    for part in (one, two):
        sides = sides + part[:EIG, :].astype(jnp.float32)
    inv = root[0:1, :]
    value = inv * (own[...] * inv + 0.5 * sides)
    mixed[...] = value
    total = lax.dot_general(
        value, value, NT, precision=lax.Precision.HIGHEST, preferred_element_type=jnp.float32
    )
    gram[...] = jnp.concatenate([total[: EIG // 2], total[EIG // 2 :]], axis=1)


def solve_kernel(factor, gram, mixed, out):
    rows = lax.broadcasted_iota(jnp.int32, (EIG, 2 * EIG), 0)
    lanes = lax.broadcasted_iota(jnp.int32, (EIG, 2 * EIG), 1)
    unit = (rows + EIG == lanes).astype(jnp.float32)
    square = jnp.concatenate([gram[:, :EIG], gram[:, EIG:]], axis=0)
    work = jnp.concatenate([square, jnp.zeros((EIG, EIG), jnp.float32)], axis=1) + unit
    done = []
    for at in range(0, EIG, 8):
        wide = [jnp.broadcast_to(work[:, at + j : at + j + 1], (EIG - at, 2 * EIG)) for j in range(8)]
        for j in range(8):
            root = lax.rsqrt(wide[j][j : j + 1, :])
            pivot = work[j : j + 1, :] * root
            done.append(pivot)
            lower = wide[j] * root
            work = work - lower * pivot
            for other in range(j + 1, 8):
                wide[other] = wide[other] - lower * (wide[other][j : j + 1, :] * root)
        work = work[8:]
    inverse = jnp.concatenate(done, axis=0)[:, EIG:]
    out[...] = factor * jnp.dot(
        inverse, mixed[...], precision=lax.Precision.HIGHEST, preferred_element_type=jnp.float32
    )


def local(features, scales, neighbor_lists, eigen_block):
    sub = lax.axis_index("sub").astype(jnp.int32)
    half = (neighbor_lists.shape[0] - 1) // 2
    total_rows = ROWS * lax.axis_size("blk") * lax.axis_size("sub")
    sub_arg = sub.reshape(1)

    block_scales = scales.astype(jnp.float32)
    own_lists = lax.dynamic_slice_in_dim(neighbor_lists, sub * ROWS, ROWS, axis=2)
    first, second = call(
        functools.partial(pack_kernel, half),
        (bf16(ROWS + EXTRA, F),) * 2,
        specs=(SMEM, VMEM, VMEM, VMEM),
    )(sub_arg, features, block_scales, own_lists)

    first, second, ready, all_lists = lax.optimization_barrier(
        (first, second, features, neighbor_lists)
    )
    first = moved(first, *BAND[0])
    second = moved(second, *BAND[1])
    slot2 = moved(ready, 0, 2)
    slot1 = moved(ready, 0, 1)
    slot3 = moved(slot2, 0, 1)
    block = (features, slot1, slot2, slot3)

    tile_outs = (bf16(ROWS, SLOTS * ROWS), f32(SLOTS, ROWS), f32(1, ROWS))
    scratch = (
        pltpu.VMEM((SLOTS, ROWS, ROWS), jnp.float32),
        pltpu.VMEM((ROWS, 128), jnp.int32),
        pltpu.VMEM((ROWS, 128), jnp.float32),
    )

    def listed(d):
        return pl.BlockSpec((1, NNB, SLOTS * ROWS), lambda i: (half + d, 0, 0))

    def band_tile(index, moving, row, tokens=(), flops=1000):
        d, u = BAND[index]
        body = functools.partial(band_tile_kernel, u, 1 + index // 2)
        specs = (SMEM,) + (VMEM,) * 8 + (HBM,) * len(tokens) + (listed(d),)
        args = (sub_arg, *block, moving, norms, block_scales, row, *tokens, all_lists)
        tile, row, col = call(body, tile_outs, scratch, specs, flops)(*args)
        return tile, row, moved(col, -d, u)

    tile0, row, col0, norms = call(
        own_tile_kernel,
        tile_outs + (f32(SLOTS, ROWS),),
        scratch,
        (SMEM,) + (VMEM,) * 5 + (listed(0),),
    )(sub_arg, *block, block_scales, all_lists)
    first, second, row = lax.optimization_barrier((first, second, row))
    third = moved(first, *ONWARD[0])
    fourth = moved(second, *ONWARD[1])
    tile1, row, col1 = band_tile(0, first, row)
    tile2, row, col2 = band_tile(1, second, row)
    tile3, row, col3 = band_tile(2, third, row)
    tile4, row, col4 = band_tile(3, fourth, row, (col1, col2), 4 * 10**9)
    tiles = (tile0, tile1, tile2, tile3, tile4)

    pair = row[0:2] + moved(row[2:4], 0, 2)
    own = pair[0:1] + moved(pair[1:2], 0, 1)
    root = lax.rsqrt(1.0 + 0.5 * (own + col0 + col1 + col2 + col3 + col4))
    scaled_low = (eigen_block * root).astype(jnp.bfloat16)
    pair = jnp.concatenate([scaled_low, moved(scaled_low, 0, 1)], axis=0)
    one, two = routed((pair, pair))
    far = moved(pair, 0, 2)
    swapped = moved(jnp.concatenate([one[EIG:], two[EIG:]], axis=0), 0, 1)

    with_sub = (SMEM,) + (VMEM,) * 8
    z_outs = (f32(EIG, ROWS), bf16(2 * EIG, ROWS), bf16(2 * EIG, ROWS))
    z0, keep, give = call(col_kernel, z_outs, specs=with_sub)(
        sub_arg, scaled_low, pair[EIG:], far, *tiles
    )
    taken = moved(give, 0, 1)
    one_back, two_back = routed(
        (
            jnp.concatenate([keep[:EIG], taken[:EIG]], axis=0),
            jnp.concatenate([keep[EIG:], taken[EIG:]], axis=0),
        ),
        back=True,
    )
    swapped, _ = lax.optimization_barrier((swapped, z0))
    y_outs = (f32(EIG, 2 * ROWS), bf16(EIG, 2 * ROWS))
    kept, sent = call(row_kernel, y_outs, specs=with_sub + (VMEM,))(
        sub_arg, scaled_low, one, two, swapped, *tiles
    )
    got = moved(sent, 0, 2)
    owed = kept[:, ROWS:] + got[:, ROWS:].astype(jnp.float32)
    owed = owed + one_back[EIG:].astype(jnp.float32) + two_back[EIG:].astype(jnp.float32)
    mixed, gram = call(mix_kernel, (f32(EIG, ROWS), f32(EIG // 2, 2 * EIG)))(
        eigen_block, root, kept, got, one_back, two_back, z0, moved(owed, 0, 1)
    )
    n_blk, n_sub = lax.axis_size("blk"), lax.axis_size("sub")
    for partners in ROUNDS:
        parts = [gram]
        for flip_blk, flip_sub in partners:
            pairs = [
                (b * n_sub + s, (b ^ flip_blk) * n_sub + (s ^ flip_sub))
                for b in range(n_blk)
                for s in range(n_sub)
            ]
            parts.append(lax.ppermute(gram, ("blk", "sub"), pairs))
        gram = functools.reduce(jnp.add, parts)
    body = functools.partial(solve_kernel, math.sqrt(total_rows))
    return call(body, f32(EIG, ROWS))(gram, mixed)


def solution(mesh):
    placed = (P(("blk", "sub"), None), P("blk"), P(None, None, "blk"), P(None, ("blk", "sub")))
    return jax.shard_map(
        local, mesh=mesh, in_specs=placed, out_specs=P(None, ("blk", "sub")), check_vma=False
    )
```

```python
import functools
import math

import jax
import jax.numpy as jnp
from jax import lax
from jax.experimental import pallas as pl
from jax.experimental.pallas import tpu as pltpu
from jax.sharding import PartitionSpec as P

F = 768
ROWS = 384
SLOTS = 4
EIG = 64
NNB = 16
BAND = ((2, 0), (-1, 2), (4, 0), (-3, 2))
ROUTES = ((BAND[2], BAND[3]), (BAND[0], BAND[1]))
ONWARD = ((2, 0), (-2, 0))
EXTRA = 2 * NNB
ROUNDS = (((0, 1),), ((0, 2), (1, 0), (1, 2)), ((2, 0), (4, 0), (6, 0)), ((8, 0), (16, 0), (24, 0)))
FOLDED = 2.0 * math.log2(math.e) / F
NT = (((1,), (1,)), ((), ()))
LIMIT = 24 * 1024 * 1024


def moved(value, blocks, flip):
    n_blk, n_sub = lax.axis_size("blk"), lax.axis_size("sub")
    pairs = [
        (b * n_sub + s, ((b + blocks) % n_blk) * n_sub + (s ^ flip))
        for b in range(n_blk)
        for s in range(n_sub)
    ]
    return lax.ppermute(value, ("blk", "sub"), pairs)


def routed(value, back=False):
    n_blk, n_sub = lax.axis_size("blk"), lax.axis_size("sub")
    outs = []
    for part, routes in zip(value, ROUTES):
        pairs = []
        for b in range(n_blk):
            for s in range(n_sub):
                d, flip = routes[s % 2]
                pairs.append((b * n_sub + s, ((b - d if back else b + d) % n_blk) * n_sub + (s ^ flip)))
        outs.append(lax.ppermute(part, ("blk", "sub"), pairs))
    return outs


VMEM = pl.BlockSpec(memory_space=pltpu.VMEM)
SMEM = pl.BlockSpec(memory_space=pltpu.SMEM)
HBM = pl.BlockSpec(memory_space=pltpu.HBM)


def call(body, outs, scratch=(), specs=None, flops=1000):
    def run(*args):
        return pl.pallas_call(
            body,
            grid=(1,),
            out_shape=outs,
            in_specs=list(specs) if specs else [VMEM] * len(args),
            out_specs=jax.tree.map(lambda _: VMEM, outs),
            scratch_shapes=list(scratch),
            compiler_params=pltpu.CompilerParams(vmem_limit_bytes=LIMIT),
            cost_estimate=pl.CostEstimate(flops=flops, bytes_accessed=1000, transcendentals=0),
        )(*args)

    return run


def f32(*shape):
    return jax.ShapeDtypeStruct(shape, jnp.float32)


def bf16(*shape):
    return jax.ShapeDtypeStruct(shape, jnp.bfloat16)


def own_tile_kernel(sub, f0, f1, f2, f3, scales, lists, tile, row, col, norms, inner, words, cols):
    ones = jnp.ones((8, F), jnp.bfloat16)
    for slot, ref in enumerate((f0, f1, f2, f3)):
        value = ref[...].astype(jnp.float32)
        square = value * value
        high = square.astype(jnp.bfloat16)
        low = (square - high.astype(jnp.float32)).astype(jnp.bfloat16)
        total = lax.dot_general(ones, high, NT, preferred_element_type=jnp.float32)
        total = total + lax.dot_general(ones, low, NT, preferred_element_type=jnp.float32)
        norms[slot : slot + 1, :] = total[0:1, :]
    tile_kernel(0, 0, sub, f0, f1, f2, f3, f0, norms, scales, None, lists, tile, row, col, inner, words, cols)


def band_tile_kernel(flip, reverse, sub, *refs):
    tile_kernel(flip, reverse, sub, *refs[:8], *refs[-7:])


def pack_kernel(half, sub, features, scales, lists, first, second):
    at = pl.multiple_of(sub[0] * ROWS, 128)
    scale = jnp.concatenate([scales[pl.ds(at, ROWS)].reshape(1, ROWS), jnp.ones((1, ROWS), jnp.float32)], axis=1)
    scale = jnp.broadcast_to(scale, (NNB, 2 * ROWS)).astype(jnp.bfloat16)
    for out, chosen in ((first, BAND[0::2]), (second, BAND[1::2])):
        out[:ROWS, :] = features[...]
        position = jnp.concatenate([lists[half - d] for d, _ in chosen], axis=1)
        group = position >> 7
        code = jnp.left_shift(128 + (position & 127), group & 7)
        code = jnp.where(group >= 8, -code, code)
        out[ROWS : ROWS + NNB, :] = code.astype(jnp.float32).astype(jnp.bfloat16)
        out[ROWS + NNB :, :] = scale


def tile_kernel(flip, reverse, sub, f0, f1, f2, f3, moving, norms, scales, before, lists, tile, row, col, inner, words, cols):
    me = sub[0]
    feats = moving[:ROWS, :].astype(jnp.float32)
    half_norm = 0.5 * jnp.sum(feats * feats, axis=1, keepdims=True)

    if reverse:
        code = moving[ROWS : ROWS + NNB, (reverse - 1) * ROWS : reverse * ROWS].astype(jnp.float32)
        code = code.astype(jnp.int32)
        size = jnp.abs(code)
        power = jnp.zeros_like(size)
        for bit in range(1, 8):
            power = power + (size >= (128 << bit)).astype(jnp.int32)
        lane = (size >> power) - 128
        group = power + jnp.where(code < 0, 8, 0)
        slice_at = (group * 11) >> 5
        group = (slice_at ^ me) * 3 + group - 3 * slice_at
        pieces = [lane.astype(jnp.float32), jnp.left_shift(1, group).astype(jnp.float32)]
        own_scale = moving[ROWS + NNB :, :ROWS].astype(jnp.float32)[0:1]
    else:
        pieces = [jnp.zeros((32, ROWS), jnp.float32)]
        own_scale = scales[pl.ds(pl.multiple_of(me * ROWS, 128), ROWS)].reshape(1, ROWS)
    stacked = jnp.concatenate(
        pieces + [FOLDED / own_scale, jnp.zeros((95, ROWS), jnp.float32)], axis=0
    )
    turned = stacked.T
    move_scale = turned[:, 32:33]
    if reverse:
        sublane = lax.broadcasted_iota(jnp.int32, (128, ROWS), 0).astype(jnp.float32)
        word = jnp.zeros((128, ROWS), jnp.float32)
        for m in range(NNB):
            word = word + jnp.where(pieces[0][m : m + 1, :] == sublane, pieces[1][m : m + 1, :], 0.0)
        words[...] = word.T.astype(jnp.int32)

    row_at = lax.broadcasted_iota(jnp.int32, (8, ROWS), 0)
    for slot, ref in enumerate((f0, f1, f2, f3)):
        inner[slot] = lax.dot_general(moving[:ROWS, :], ref[...], NT, preferred_element_type=jnp.float32)
        start = pl.multiple_of((me ^ slot) * ROWS, 128)
        listed = lists[0, :, pl.ds(start, ROWS)] - (me ^ flip) * ROWS
        inside = (listed >= 0) & (listed < ROWS)
        sublane = listed & 7
        bit = jnp.where(inside, listed >> 3, 0)
        first = jnp.where(inside & (bit < 24), jnp.left_shift(1, bit), 0)
        second = jnp.where(inside & (bit >= 24), jnp.left_shift(1, jnp.maximum(bit - 24, 0)), 0)
        low = jnp.zeros((8, ROWS), jnp.int32)
        high = jnp.zeros((8, ROWS), jnp.int32)
        for m in range(NNB):
            same = sublane[m : m + 1, :] == row_at
            low = low | jnp.where(same, first[m : m + 1, :], 0)
            high = high | jnp.where(same, second[m : m + 1, :], 0)
        norm = 0.5 * norms[slot : slot + 1, :]
        scale = 1.0 / scales[pl.ds(start, ROWS)].reshape(1, ROWS)
        row_sum = jnp.zeros((8, ROWS), jnp.float32)
        step = 32
        for at in range(0, ROWS, step):
            source = low if at < 192 else high
            counts = [
                (source >> ((at // 8 + c) % 24)) & 1 for c in range(step // 8)
            ]
            count = jnp.concatenate(counts, axis=0)
            if reverse:
                word = words[at : at + step, :]
                count = count + jnp.concatenate(
                    [(word >> (3 * slot + g)) & 1 for g in range(3)], axis=1
                )
            power = inner[slot, at : at + step, :] - half_norm[at : at + step] - norm
            power = power * move_scale[at : at + step] * scale
            weight = jnp.exp2(power) * count.astype(jnp.float32)
            tile[at : at + step, slot * ROWS : (slot + 1) * ROWS] = weight.astype(jnp.bfloat16)
            for c in range(step // 8):
                row_sum = row_sum + weight[8 * c : 8 * c + 8, :]
            lanes = weight[:, 0:128] + weight[:, 128:256] + weight[:, 256:384]
            if slot == 0:
                cols[at : at + step, :] = lanes
            else:
                cols[at : at + step, :] = cols[at : at + step, :] + lanes
        total = jnp.sum(row_sum, axis=0, keepdims=True)
        row[slot : slot + 1, :] = before[slot : slot + 1, :] + total if reverse else total
    col[...] = jnp.sum(cols[...].T, axis=0, keepdims=True)


def col_kernel(sub, x0, x1, far, t0, t1, t2, t3, t4, z0, keep, give):
    block = jnp.concatenate([x0[...], x1[...], far[:EIG, :], far[EIG:, :]], axis=1)
    z1, z2, z3, z4 = [
        lax.dot_general(block, tile[...], NT, preferred_element_type=jnp.float32)
        for tile in (t1, t2, t3, t4)
    ]
    odd = sub[0] % 2 == 1
    for at, (even_one, odd_one) in ((0, (z3, z4)), (EIG, (z1, z2))):
        keep[at : at + EIG, :] = jnp.where(odd, odd_one, even_one).astype(jnp.bfloat16)
        give[at : at + EIG, :] = jnp.where(odd, even_one, odd_one).astype(jnp.bfloat16)
    z0[...] = lax.dot_general(block, t0[...], NT, preferred_element_type=jnp.float32)


def row_kernel(sub, x0, one, two, got, t0, t1, t2, t3, t4, kept, sent):
    odd = sub[0] % 2 == 1
    one_x, two_x = one[:EIG, :].astype(jnp.float32), two[:EIG, :].astype(jnp.float32)
    got_one, got_two = got[:EIG, :].astype(jnp.float32), got[EIG:, :].astype(jnp.float32)
    x1 = jnp.where(odd, got_two, two_x).astype(jnp.bfloat16)
    x2 = jnp.where(odd, two_x, got_two).astype(jnp.bfloat16)
    x3 = jnp.where(odd, got_one, one_x).astype(jnp.bfloat16)
    x4 = jnp.where(odd, one_x, got_one).astype(jnp.bfloat16)
    for half, out in ((1, sent), (0, kept)):
        at = half * 2 * ROWS
        total = jnp.zeros((EIG, 2 * ROWS), jnp.float32)
        for vectors, tile in ((x0[...], t0), (x1, t1), (x2, t2), (x3, t3), (x4, t4)):
            total = total + jnp.dot(
                vectors, tile[:, at : at + 2 * ROWS], preferred_element_type=jnp.float32
            )
        out[...] = total.astype(out.dtype)


def mix_kernel(own, root, kept, got, one, two, z0, swapped, mixed, gram):
    sides = kept[:, :ROWS] + got[:, :ROWS].astype(jnp.float32) + z0[...] + swapped[...]
    for part in (one, two):
        sides = sides + part[:EIG, :].astype(jnp.float32)
    inv = root[0:1, :]
    value = inv * (own[...] * inv + 0.5 * sides)
    mixed[...] = value
    total = lax.dot_general(
        value, value, NT, precision=lax.Precision.HIGHEST, preferred_element_type=jnp.float32
    )
    gram[...] = jnp.concatenate([total[: EIG // 2], total[EIG // 2 :]], axis=1)


def solve_kernel(factor, gram, mixed, out):
    rows = lax.broadcasted_iota(jnp.int32, (EIG, 2 * EIG), 0)
    lanes = lax.broadcasted_iota(jnp.int32, (EIG, 2 * EIG), 1)
    unit = (rows + EIG == lanes).astype(jnp.float32)
    square = jnp.concatenate([gram[:, :EIG], gram[:, EIG:]], axis=0)
    work = jnp.concatenate([square, jnp.zeros((EIG, EIG), jnp.float32)], axis=1) + unit
    done = []
    for at in range(0, EIG, 8):
        wide = [jnp.broadcast_to(work[:, at + j : at + j + 1], (EIG - at, 2 * EIG)) for j in range(8)]
        for j in range(8):
            root = lax.rsqrt(wide[j][j : j + 1, :])
            pivot = work[j : j + 1, :] * root
            done.append(pivot)
            lower = wide[j] * root
            work = work - lower * pivot
            for other in range(j + 1, 8):
                wide[other] = wide[other] - lower * (wide[other][j : j + 1, :] * root)
        work = work[8:]
    inverse = jnp.concatenate(done, axis=0)[:, EIG:]
    out[...] = factor * jnp.dot(
        inverse, mixed[...], precision=lax.Precision.HIGHEST, preferred_element_type=jnp.float32
    )


def local(features, scales, neighbor_lists, eigen_block):
    sub = lax.axis_index("sub").astype(jnp.int32)
    half = (neighbor_lists.shape[0] - 1) // 2
    total_rows = ROWS * lax.axis_size("blk") * lax.axis_size("sub")
    sub_arg = sub.reshape(1)

    block_scales = scales.astype(jnp.float32)
    own_lists = lax.dynamic_slice_in_dim(neighbor_lists, sub * ROWS, ROWS, axis=2)
    first, second = call(
        functools.partial(pack_kernel, half),
        (bf16(ROWS + EXTRA, F),) * 2,
        specs=(SMEM, VMEM, VMEM, VMEM),
    )(sub_arg, features, block_scales, own_lists)

    first, second, ready, all_lists = lax.optimization_barrier(
        (first, second, features, neighbor_lists)
    )
    first = moved(first, *BAND[0])
    second = moved(second, *BAND[1])
    slot2 = moved(ready, 0, 2)
    slot1 = moved(ready, 0, 1)
    slot3 = moved(slot2, 0, 1)
    block = (features, slot1, slot2, slot3)

    tile_outs = (bf16(ROWS, SLOTS * ROWS), f32(SLOTS, ROWS), f32(1, ROWS))
    scratch = (
        pltpu.VMEM((SLOTS, ROWS, ROWS), jnp.float32),
        pltpu.VMEM((ROWS, 128), jnp.int32),
        pltpu.VMEM((ROWS, 128), jnp.float32),
    )

    def listed(d):
        return pl.BlockSpec((1, NNB, SLOTS * ROWS), lambda i: (half + d, 0, 0))

    def band_tile(index, moving, row, tokens=(), flops=1000):
        d, u = BAND[index]
        body = functools.partial(band_tile_kernel, u, 1 + index // 2)
        specs = (SMEM,) + (VMEM,) * 8 + (HBM,) * len(tokens) + (listed(d),)
        args = (sub_arg, *block, moving, norms, block_scales, row, *tokens, all_lists)
        tile, row, col = call(body, tile_outs, scratch, specs, flops)(*args)
        return tile, row, moved(col, -d, u)

    tile0, row, col0, norms = call(
        own_tile_kernel,
        tile_outs + (f32(SLOTS, ROWS),),
        scratch,
        (SMEM,) + (VMEM,) * 5 + (listed(0),),
    )(sub_arg, *block, block_scales, all_lists)
    first, second, row = lax.optimization_barrier((first, second, row))
    third = moved(first, *ONWARD[0])
    fourth = moved(second, *ONWARD[1])
    tile1, row, col1 = band_tile(0, first, row)
    tile2, row, col2 = band_tile(1, second, row)
    tile3, row, col3 = band_tile(2, third, row)
    tile4, row, col4 = band_tile(3, fourth, row, (col1, col2), 4 * 10**9)
    tiles = (tile0, tile1, tile2, tile3, tile4)

    pair = row[0:2] + moved(row[2:4], 0, 2)
    own = pair[0:1] + moved(pair[1:2], 0, 1)
    root = lax.rsqrt(1.0 + 0.5 * (own + col0 + col1 + col2 + col3 + col4))
    scaled_low = (eigen_block * root).astype(jnp.bfloat16)
    pair = jnp.concatenate([scaled_low, moved(scaled_low, 0, 1)], axis=0)
    one, two = routed((pair, pair))
    far = moved(pair, 0, 2)

    with_sub = (SMEM,) + (VMEM,) * 8
    z_outs = (f32(EIG, ROWS), bf16(2 * EIG, ROWS), bf16(2 * EIG, ROWS))
    z0, keep, give = call(col_kernel, z_outs, specs=with_sub)(
        sub_arg, scaled_low, pair[EIG:], far, *tiles
    )
    taken = moved(give, 0, 1)
    one_back, two_back = routed(
        (
            jnp.concatenate([keep[:EIG], taken[:EIG]], axis=0),
            jnp.concatenate([keep[EIG:], taken[EIG:]], axis=0),
        ),
        back=True,
    )
    one, two, _ = lax.optimization_barrier((one, two, z0))
    swapped = moved(jnp.concatenate([one[EIG:], two[EIG:]], axis=0), 0, 1)
    y_outs = (f32(EIG, 2 * ROWS), bf16(EIG, 2 * ROWS))
    kept, sent = call(row_kernel, y_outs, specs=with_sub + (VMEM,))(
        sub_arg, scaled_low, one, two, swapped, *tiles
    )
    got = moved(sent, 0, 2)
    owed = kept[:, ROWS:] + got[:, ROWS:].astype(jnp.float32)
    owed = owed + one_back[EIG:].astype(jnp.float32) + two_back[EIG:].astype(jnp.float32)
    mixed, gram = call(mix_kernel, (f32(EIG, ROWS), f32(EIG // 2, 2 * EIG)))(
        eigen_block, root, kept, got, one_back, two_back, z0, moved(owed, 0, 1)
    )
    n_blk, n_sub = lax.axis_size("blk"), lax.axis_size("sub")
    for partners in ROUNDS:
        parts = [gram]
        for flip_blk, flip_sub in partners:
            pairs = [
                (b * n_sub + s, (b ^ flip_blk) * n_sub + (s ^ flip_sub))
                for b in range(n_blk)
                for s in range(n_sub)
            ]
            parts.append(lax.ppermute(gram, ("blk", "sub"), pairs))
        gram = functools.reduce(jnp.add, parts)
    body = functools.partial(solve_kernel, math.sqrt(total_rows))
    return call(body, f32(EIG, ROWS))(gram, mixed)


def solution(mesh):
    placed = (P(("blk", "sub"), None), P("blk"), P(None, None, "blk"), P(None, ("blk", "sub")))
    return jax.shard_map(
        local, mesh=mesh, in_specs=placed, out_specs=P(None, ("blk", "sub")), check_vma=False
    )
```

```python
import functools
import math

import jax
import jax.numpy as jnp
from jax import lax
from jax.experimental import pallas as pl
from jax.experimental.pallas import tpu as pltpu
from jax.sharding import PartitionSpec as P

F = 768
ROWS = 384
SLOTS = 4
EIG = 64
NNB = 16
BAND = ((2, 0), (-1, 2), (4, 0), (-3, 2))
ROUTES = ((BAND[2], BAND[3]), (BAND[0], BAND[1]))
ONWARD = ((2, 0), (-2, 0))
EXTRA = 2 * NNB
ROUNDS = (((0, 1),), ((0, 2), (1, 0), (1, 2)), ((2, 0), (4, 0), (6, 0)), ((8, 0), (16, 0), (24, 0)))
FOLDED = 2.0 * math.log2(math.e) / F
NT = (((1,), (1,)), ((), ()))
LIMIT = 24 * 1024 * 1024


def moved(value, blocks, flip):
    n_blk, n_sub = lax.axis_size("blk"), lax.axis_size("sub")
    pairs = [
        (b * n_sub + s, ((b + blocks) % n_blk) * n_sub + (s ^ flip))
        for b in range(n_blk)
        for s in range(n_sub)
    ]
    return lax.ppermute(value, ("blk", "sub"), pairs)


def routed(value, back=False):
    n_blk, n_sub = lax.axis_size("blk"), lax.axis_size("sub")
    outs = []
    for part, routes in zip(value, ROUTES):
        pairs = []
        for b in range(n_blk):
            for s in range(n_sub):
                d, flip = routes[s % 2]
                pairs.append((b * n_sub + s, ((b - d if back else b + d) % n_blk) * n_sub + (s ^ flip)))
        outs.append(lax.ppermute(part, ("blk", "sub"), pairs))
    return outs


VMEM = pl.BlockSpec(memory_space=pltpu.VMEM)
SMEM = pl.BlockSpec(memory_space=pltpu.SMEM)
HBM = pl.BlockSpec(memory_space=pltpu.HBM)


def call(body, outs, scratch=(), specs=None, flops=1000):
    def run(*args):
        return pl.pallas_call(
            body,
            grid=(1,),
            out_shape=outs,
            in_specs=list(specs) if specs else [VMEM] * len(args),
            out_specs=jax.tree.map(lambda _: VMEM, outs),
            scratch_shapes=list(scratch),
            compiler_params=pltpu.CompilerParams(vmem_limit_bytes=LIMIT),
            cost_estimate=pl.CostEstimate(flops=flops, bytes_accessed=1000, transcendentals=0),
        )(*args)

    return run


def f32(*shape):
    return jax.ShapeDtypeStruct(shape, jnp.float32)


def bf16(*shape):
    return jax.ShapeDtypeStruct(shape, jnp.bfloat16)


def own_tile_kernel(sub, f0, f1, f2, f3, scales, lists, tile, row, col, norms, inner, words, cols):
    ones = jnp.ones((8, F), jnp.bfloat16)
    for slot, ref in enumerate((f0, f1, f2, f3)):
        value = ref[...].astype(jnp.float32)
        square = value * value
        high = square.astype(jnp.bfloat16)
        low = (square - high.astype(jnp.float32)).astype(jnp.bfloat16)
        total = lax.dot_general(ones, high, NT, preferred_element_type=jnp.float32)
        total = total + lax.dot_general(ones, low, NT, preferred_element_type=jnp.float32)
        norms[slot : slot + 1, :] = total[0:1, :]
    tile_kernel(0, 0, sub, f0, f1, f2, f3, f0, norms, scales, None, lists, tile, row, col, inner, words, cols)


def band_tile_kernel(flip, reverse, sub, *refs):
    tile_kernel(flip, reverse, sub, *refs[:8], *refs[-7:])


def pack_kernel(half, sub, features, scales, lists, first, second):
    at = pl.multiple_of(sub[0] * ROWS, 128)
    scale = jnp.concatenate([scales[pl.ds(at, ROWS)].reshape(1, ROWS), jnp.ones((1, ROWS), jnp.float32)], axis=1)
    scale = jnp.broadcast_to(scale, (NNB, 2 * ROWS)).astype(jnp.bfloat16)
    for out, chosen in ((first, BAND[0::2]), (second, BAND[1::2])):
        out[:ROWS, :] = features[...]
        position = jnp.concatenate([lists[half - d] for d, _ in chosen], axis=1)
        group = position >> 7
        code = jnp.left_shift(128 + (position & 127), group & 7)
        code = jnp.where(group >= 8, -code, code)
        out[ROWS : ROWS + NNB, :] = code.astype(jnp.float32).astype(jnp.bfloat16)
        out[ROWS + NNB :, :] = scale


def tile_kernel(flip, reverse, sub, f0, f1, f2, f3, moving, norms, scales, before, lists, tile, row, col, inner, words, cols):
    me = sub[0]
    feats = moving[:ROWS, :].astype(jnp.float32)
    half_norm = 0.5 * jnp.sum(feats * feats, axis=1, keepdims=True)

    if reverse:
        code = moving[ROWS : ROWS + NNB, (reverse - 1) * ROWS : reverse * ROWS].astype(jnp.float32)
        code = code.astype(jnp.int32)
        size = jnp.abs(code)
        power = jnp.zeros_like(size)
        for bit in range(1, 8):
            power = power + (size >= (128 << bit)).astype(jnp.int32)
        lane = (size >> power) - 128
        group = power + jnp.where(code < 0, 8, 0)
        slice_at = (group * 11) >> 5
        group = (slice_at ^ me) * 3 + group - 3 * slice_at
        pieces = [lane.astype(jnp.float32), jnp.left_shift(1, group).astype(jnp.float32)]
        own_scale = moving[ROWS + NNB :, :ROWS].astype(jnp.float32)[0:1]
    else:
        pieces = [jnp.zeros((32, ROWS), jnp.float32)]
        own_scale = scales[pl.ds(pl.multiple_of(me * ROWS, 128), ROWS)].reshape(1, ROWS)
    stacked = jnp.concatenate(
        pieces + [FOLDED / own_scale, jnp.zeros((95, ROWS), jnp.float32)], axis=0
    )
    turned = stacked.T
    move_scale = turned[:, 32:33]
    if reverse:
        sublane = lax.broadcasted_iota(jnp.int32, (128, ROWS), 0).astype(jnp.float32)
        word = jnp.zeros((128, ROWS), jnp.float32)
        for m in range(NNB):
            word = word + jnp.where(pieces[0][m : m + 1, :] == sublane, pieces[1][m : m + 1, :], 0.0)
        words[...] = word.T.astype(jnp.int32)

    row_at = lax.broadcasted_iota(jnp.int32, (8, ROWS), 0)
    for slot, ref in enumerate((f0, f1, f2, f3)):
        inner[slot] = lax.dot_general(moving[:ROWS, :], ref[...], NT, preferred_element_type=jnp.float32)
        start = pl.multiple_of((me ^ slot) * ROWS, 128)
        listed = lists[0, :, pl.ds(start, ROWS)] - (me ^ flip) * ROWS
        inside = (listed >= 0) & (listed < ROWS)
        sublane = listed & 7
        bit = jnp.where(inside, listed >> 3, 0)
        first = jnp.where(inside & (bit < 24), jnp.left_shift(1, bit), 0)
        second = jnp.where(inside & (bit >= 24), jnp.left_shift(1, jnp.maximum(bit - 24, 0)), 0)
        low = jnp.zeros((8, ROWS), jnp.int32)
        high = jnp.zeros((8, ROWS), jnp.int32)
        for m in range(NNB):
            same = sublane[m : m + 1, :] == row_at
            low = low | jnp.where(same, first[m : m + 1, :], 0)
            high = high | jnp.where(same, second[m : m + 1, :], 0)
        norm = 0.5 * norms[slot : slot + 1, :]
        scale = 1.0 / scales[pl.ds(start, ROWS)].reshape(1, ROWS)
        row_sum = jnp.zeros((8, ROWS), jnp.float32)
        step = 32
        for at in range(0, ROWS, step):
            source = low if at < 192 else high
            counts = [
                (source >> ((at // 8 + c) % 24)) & 1 for c in range(step // 8)
            ]
            count = jnp.concatenate(counts, axis=0)
            if reverse:
                word = words[at : at + step, :]
                count = count + jnp.concatenate(
                    [(word >> (3 * slot + g)) & 1 for g in range(3)], axis=1
                )
            power = inner[slot, at : at + step, :] - half_norm[at : at + step] - norm
            power = power * move_scale[at : at + step] * scale
            weight = jnp.exp2(power) * count.astype(jnp.float32)
            tile[at : at + step, slot * ROWS : (slot + 1) * ROWS] = weight.astype(jnp.bfloat16)
            for c in range(step // 8):
                row_sum = row_sum + weight[8 * c : 8 * c + 8, :]
            lanes = weight[:, 0:128] + weight[:, 128:256] + weight[:, 256:384]
            if slot == 0:
                cols[at : at + step, :] = lanes
            else:
                cols[at : at + step, :] = cols[at : at + step, :] + lanes
        total = jnp.sum(row_sum, axis=0, keepdims=True)
        row[slot : slot + 1, :] = before[slot : slot + 1, :] + total if reverse else total
    col[...] = jnp.sum(cols[...].T, axis=0, keepdims=True)


def col_kernel(sub, x0, x1, far, t0, t1, t2, t3, t4, z0, keep, give):
    block = jnp.concatenate([x0[...], x1[...], far[:EIG, :], far[EIG:, :]], axis=1)
    z1, z2, z3, z4 = [
        lax.dot_general(block, tile[...], NT, preferred_element_type=jnp.float32)
        for tile in (t1, t2, t3, t4)
    ]
    odd = sub[0] % 2 == 1
    for at, (even_one, odd_one) in ((0, (z3, z4)), (EIG, (z1, z2))):
        keep[at : at + EIG, :] = jnp.where(odd, odd_one, even_one).astype(jnp.bfloat16)
        give[at : at + EIG, :] = jnp.where(odd, even_one, odd_one).astype(jnp.bfloat16)
    z0[...] = lax.dot_general(block, t0[...], NT, preferred_element_type=jnp.float32)


def row_kernel(sub, x0, one, two, got, t0, t1, t2, t3, t4, kept, sent):
    odd = sub[0] % 2 == 1
    one_x, two_x = one[:EIG, :].astype(jnp.float32), two[:EIG, :].astype(jnp.float32)
    got_one, got_two = got[:EIG, :].astype(jnp.float32), got[EIG:, :].astype(jnp.float32)
    x1 = jnp.where(odd, got_two, two_x).astype(jnp.bfloat16)
    x2 = jnp.where(odd, two_x, got_two).astype(jnp.bfloat16)
    x3 = jnp.where(odd, got_one, one_x).astype(jnp.bfloat16)
    x4 = jnp.where(odd, one_x, got_one).astype(jnp.bfloat16)
    for half, out in ((1, sent), (0, kept)):
        at = half * 2 * ROWS
        total = jnp.zeros((EIG, 2 * ROWS), jnp.float32)
        for vectors, tile in ((x0[...], t0), (x1, t1), (x2, t2), (x3, t3), (x4, t4)):
            total = total + jnp.dot(
                vectors, tile[:, at : at + 2 * ROWS], preferred_element_type=jnp.float32
            )
        out[...] = total.astype(out.dtype)


def mix_kernel(own, root, kept, got, one, two, z0, swapped, mixed, gram):
    sides = kept[:, :ROWS] + got[:, :ROWS].astype(jnp.float32) + z0[...] + swapped[...]
    for part in (one, two):
        sides = sides + part[:EIG, :].astype(jnp.float32)
    inv = root[0:1, :]
    value = inv * (own[...] * inv + 0.5 * sides)
    mixed[...] = value
    total = lax.dot_general(
        value, value, NT, precision=lax.Precision.HIGHEST, preferred_element_type=jnp.float32
    )
    gram[...] = jnp.concatenate([total[: EIG // 2], total[EIG // 2 :]], axis=1)


def solve_kernel(factor, gram, mixed, out):
    rows = lax.broadcasted_iota(jnp.int32, (EIG, 2 * EIG), 0)
    lanes = lax.broadcasted_iota(jnp.int32, (EIG, 2 * EIG), 1)
    unit = (rows + EIG == lanes).astype(jnp.float32)
    square = jnp.concatenate([gram[:, :EIG], gram[:, EIG:]], axis=0)
    work = jnp.concatenate([square, jnp.zeros((EIG, EIG), jnp.float32)], axis=1) + unit
    done = []
    for at in range(0, EIG, 8):
        wide = [jnp.broadcast_to(work[:, at + j : at + j + 1], (EIG - at, 2 * EIG)) for j in range(8)]
        for j in range(8):
            root = lax.rsqrt(wide[j][j : j + 1, :])
            pivot = work[j : j + 1, :] * root
            done.append(pivot)
            lower = wide[j] * root
            work = work - lower * pivot
            for other in range(j + 1, 8):
                wide[other] = wide[other] - lower * (wide[other][j : j + 1, :] * root)
        work = work[8:]
    inverse = jnp.concatenate(done, axis=0)[:, EIG:]
    out[...] = factor * jnp.dot(
        inverse, mixed[...], precision=lax.Precision.HIGHEST, preferred_element_type=jnp.float32
    )


def local(features, scales, neighbor_lists, eigen_block):
    sub = lax.axis_index("sub").astype(jnp.int32)
    half = (neighbor_lists.shape[0] - 1) // 2
    total_rows = ROWS * lax.axis_size("blk") * lax.axis_size("sub")
    sub_arg = sub.reshape(1)

    block_scales = scales.astype(jnp.float32)
    own_lists = lax.dynamic_slice_in_dim(neighbor_lists, sub * ROWS, ROWS, axis=2)
    first, second = call(
        functools.partial(pack_kernel, half),
        (bf16(ROWS + EXTRA, F),) * 2,
        specs=(SMEM, VMEM, VMEM, VMEM),
    )(sub_arg, features, block_scales, own_lists)

    first, second, ready, all_lists = lax.optimization_barrier(
        (first, second, features, neighbor_lists)
    )
    first = moved(first, *BAND[0])
    second = moved(second, *BAND[1])
    slot2 = moved(ready, 0, 2)
    slot1 = moved(ready, 0, 1)
    slot3 = moved(slot2, 0, 1)
    block = (features, slot1, slot2, slot3)

    tile_outs = (bf16(ROWS, SLOTS * ROWS), f32(SLOTS, ROWS), f32(1, ROWS))
    scratch = (
        pltpu.VMEM((SLOTS, ROWS, ROWS), jnp.float32),
        pltpu.VMEM((ROWS, 128), jnp.int32),
        pltpu.VMEM((ROWS, 128), jnp.float32),
    )

    def listed(d):
        return pl.BlockSpec((1, NNB, SLOTS * ROWS), lambda i: (half + d, 0, 0))

    def band_tile(index, moving, row, tokens=(), flops=1000):
        d, u = BAND[index]
        body = functools.partial(band_tile_kernel, u, 1 + index // 2)
        specs = (SMEM,) + (VMEM,) * 8 + (HBM,) * len(tokens) + (listed(d),)
        args = (sub_arg, *block, moving, norms, block_scales, row, *tokens, all_lists)
        tile, row, col = call(body, tile_outs, scratch, specs, flops)(*args)
        return tile, row, moved(col, -d, u)

    tile0, row, col0, norms = call(
        own_tile_kernel,
        tile_outs + (f32(SLOTS, ROWS),),
        scratch,
        (SMEM,) + (VMEM,) * 5 + (listed(0),),
    )(sub_arg, *block, block_scales, all_lists)
    first, second, row = lax.optimization_barrier((first, second, row))
    third = moved(first, *ONWARD[0])
    fourth = moved(second, *ONWARD[1])
    tile1, row, col1 = band_tile(0, first, row)
    tile2, row, col2 = band_tile(1, second, row)
    tile3, row, col3 = band_tile(2, third, row)
    tile4, row, col4 = band_tile(3, fourth, row, (col1, col2), 4 * 10**9)
    tiles = (tile0, tile1, tile2, tile3, tile4)

    pair = row[0:2] + moved(row[2:4], 0, 2)
    own = pair[0:1] + moved(pair[1:2], 0, 1)
    root = lax.rsqrt(1.0 + 0.5 * (own + col0 + col1 + col2 + col3 + col4))
    scaled_low = (eigen_block * root).astype(jnp.bfloat16)
    pair = jnp.concatenate([scaled_low, moved(scaled_low, 0, 1)], axis=0)
    one, two = routed((pair, pair))
    far = moved(pair, 0, 2)

    with_sub = (SMEM,) + (VMEM,) * 8
    z_outs = (f32(EIG, ROWS), bf16(2 * EIG, ROWS), bf16(2 * EIG, ROWS))
    z0, keep, give = call(col_kernel, z_outs, specs=with_sub)(
        sub_arg, scaled_low, pair[EIG:], far, *tiles
    )
    taken = moved(give, 0, 1)
    one, two, _ = lax.optimization_barrier((one, two, z0))
    swapped = moved(jnp.concatenate([one[EIG:], two[EIG:]], axis=0), 0, 1)
    swapped, taken = lax.optimization_barrier((swapped, taken))
    one_back, two_back = routed(
        (
            jnp.concatenate([keep[:EIG], taken[:EIG]], axis=0),
            jnp.concatenate([keep[EIG:], taken[EIG:]], axis=0),
        ),
        back=True,
    )
    y_outs = (f32(EIG, 2 * ROWS), bf16(EIG, 2 * ROWS))
    kept, sent = call(row_kernel, y_outs, specs=with_sub + (VMEM,))(
        sub_arg, scaled_low, one, two, swapped, *tiles
    )
    got = moved(sent, 0, 2)
    owed = kept[:, ROWS:] + got[:, ROWS:].astype(jnp.float32)
    owed = owed + one_back[EIG:].astype(jnp.float32) + two_back[EIG:].astype(jnp.float32)
    mixed, gram = call(mix_kernel, (f32(EIG, ROWS), f32(EIG // 2, 2 * EIG)))(
        eigen_block, root, kept, got, one_back, two_back, z0, moved(owed, 0, 1)
    )
    n_blk, n_sub = lax.axis_size("blk"), lax.axis_size("sub")
    for partners in ROUNDS:
        parts = [gram]
        for flip_blk, flip_sub in partners:
            pairs = [
                (b * n_sub + s, (b ^ flip_blk) * n_sub + (s ^ flip_sub))
                for b in range(n_blk)
                for s in range(n_sub)
            ]
            parts.append(lax.ppermute(gram, ("blk", "sub"), pairs))
        gram = functools.reduce(jnp.add, parts)
    body = functools.partial(solve_kernel, math.sqrt(total_rows))
    return call(body, f32(EIG, ROWS))(gram, mixed)


def solution(mesh):
    placed = (P(("blk", "sub"), None), P("blk"), P(None, None, "blk"), P(None, ("blk", "sub")))
    return jax.shard_map(
        local, mesh=mesh, in_specs=placed, out_specs=P(None, ("blk", "sub")), check_vma=False
    )
```
